512 devices in a mesh: seq: 64 (over z_lo, y, core), head: 8 (over x, z_hi).
Axes of the slice: x: 4, y: 4, z: 16 (z_hi: 2, z_lo: 8; z = z_hi * 8 + z_lo), core: 2. Of those that a mesh axis runs over, the one named last changes fastest.
Arguments:
- query: bfloat16 [16384, 8192], P('seq', 'head'), may hold values from -6 to 6
- key_in: bfloat16 [16384, 1024], P('seq', 'head'), may hold values from -6 to 6
- value_input: bfloat16 [16384, 1024], P('seq', 'head'), may hold values from -6 to 6
- output_gradient: bfloat16 [16384, 8192], P('seq', 'head'), may hold values from -6 to 6
- block_order: int32 [64], replicated, may hold values from 0 to 63, each once
Outputs:
- attn_out: bfloat16 [16384, 8192], P('seq', 'head')
- d_query: bfloat16 [16384, 8192], P('seq', 'head')
- d_keyvalue: bfloat16 [2, 16384, 1024], P(None, 'seq', 'head')
- gram: float32 [8, 1024, 1024], P('head', 'seq')
The draws below stay inside these ranges and needn't reach their ends.
Inputs may be any that keep to these rules, and one draw needn't show every extreme that they name: `block_order`: each sequence block number appears once.
All inputs are finite; a program needn't handle non-finite values.
Results may differ from the reference program's by a relative error of at most 0.025.
Values may be sent and summed in bfloat16 or wider, within the bound.
No kernel may reach another device: no remote copies, remote signals or barrier semaphores. Data moves between devices by JAX's collectives and lax.ppermute only.
A program may use at most 64 MiB of HBM per device.

```python
import jax
import jax.numpy as jnp
from jax import lax

HEAD_SIZE = 128
QUERY_PER_KV = 8
TOK_DEV = 256
KEY_VALUE_HEADS = 8
GROUP_FEATURES = 1024
TOKEN_COUNT = 16384
N_SEQ = 64


def draw_query(key, part):
    key = jax.random.fold_in(key, 1)
    return jax.random.truncated_normal(key, -6.0, 6.0, (TOKEN_COUNT, KEY_VALUE_HEADS * GROUP_FEATURES), jnp.float32).astype(jnp.bfloat16)


def draw_key_in(key, part):
    key = jax.random.fold_in(key, 2)
    return jax.random.truncated_normal(key, -6.0, 6.0, (TOKEN_COUNT, KEY_VALUE_HEADS * HEAD_SIZE), jnp.float32).astype(jnp.bfloat16)


def steps_of(own_key, extent, pieces, least, top_value):
    loudness = 1.0
    for axis_at, shards_of in pieces:
        draws = jax.random.uniform(jax.random.fold_in(jax.random.fold_in(own_key, 6), axis_at), (shards_of,), jnp.float32, least / len(pieces), top_value / len(pieces))
        loudness = loudness * jnp.repeat(jnp.exp(draws), extent[axis_at] // shards_of).reshape((-1,) + (1,) * (len(extent) - 1 - axis_at))
    return loudness


def noise(own_key, dims, spread, limit, shards=(), kind=jnp.bfloat16):
    array = spread * jax.random.normal(own_key, dims, jnp.float32)
    if shards:
        array = array * steps_of(own_key, dims, shards, -0.22, 0.18)
    return jnp.clip(array, -limit, limit).astype(kind)


def setup_inputs(seed: int = 0) -> dict:
    arg_keys = jax.random.split(jax.random.key(seed), 6)
    query = draw_query(jax.random.fold_in(arg_keys[5], 71), 0)
    key_in = draw_key_in(jax.random.fold_in(arg_keys[5], 71), 0)
    value_input = noise(arg_keys[2], (TOKEN_COUNT, KEY_VALUE_HEADS * HEAD_SIZE), 1.0, 6.0, ((0, 64), (1, 8)))
    output_gradient = noise(arg_keys[3], (TOKEN_COUNT, KEY_VALUE_HEADS * GROUP_FEATURES), 1.0, 6.0, ((0, 64), (1, 8)))
    block_order = jax.random.permutation(arg_keys[4], N_SEQ).astype(jnp.int32)
    return dict(query=query, key_in=key_in, value_input=value_input, output_gradient=output_gradient, block_order=block_order)


def reference(query, key_in, value_input, output_gradient, block_order):
    scale = 1.0 / (HEAD_SIZE ** 0.5)
    n_blocks = N_SEQ
    key_value_heads = KEY_VALUE_HEADS
    offsets = jnp.arange(TOK_DEV, dtype=jnp.int32)

    def one_block(index):
        start = (index * TOK_DEV).astype(jnp.int32)
        q_blk = lax.dynamic_slice_in_dim(query, start, TOK_DEV, 0).reshape(TOK_DEV, key_value_heads, QUERY_PER_KV, HEAD_SIZE).astype(jnp.float32)
        go_blk = lax.dynamic_slice_in_dim(output_gradient, start, TOK_DEV, 0).reshape(TOK_DEV, key_value_heads, QUERY_PER_KV, HEAD_SIZE)
        q_pos = block_order[index] * TOK_DEV + offsets
        key_list = []
        value_list = []
        pos_list = []
        for step in range(3):
            source = ((index - step) % n_blocks).astype(jnp.int32)
            src_start = (source * TOK_DEV).astype(jnp.int32)
            key_list.append(lax.dynamic_slice_in_dim(key_in, src_start, TOK_DEV, 0))
            value_list.append(lax.dynamic_slice_in_dim(value_input, src_start, TOK_DEV, 0))
            pos_list.append(block_order[source] * TOK_DEV + offsets)
        all_keys = jnp.concatenate(key_list, 0).reshape(3 * TOK_DEV, key_value_heads, HEAD_SIZE).astype(jnp.float32)
        all_values = jnp.concatenate(value_list, 0).reshape(3 * TOK_DEV, key_value_heads, HEAD_SIZE)
        k_pos = jnp.concatenate(pos_list, 0)
        scores = jnp.einsum("tkgd,skd->kgts", q_blk, all_keys) * scale
        visible = k_pos[None, None, None, :] <= q_pos[None, None, :, None]
        scores = jnp.where(visible, scores, -1e30)
        top = jnp.max(scores, axis=-1, keepdims=True)
        expo = jnp.exp(scores - top)
        weights = expo / jnp.sum(expo, axis=-1, keepdims=True)
        weights_bf = weights.astype(jnp.bfloat16)
        output = jnp.einsum("kgts,skd->tkgd", weights_bf.astype(jnp.float32), all_values.astype(jnp.float32))
        out_bf = output.astype(jnp.bfloat16)
        row_dot = jnp.sum(go_blk.astype(jnp.float32) * out_bf.astype(jnp.float32), axis=-1)
        dprob = jnp.einsum("tkgd,skd->kgts", go_blk.astype(jnp.float32), all_values.astype(jnp.float32))
        dscore = (weights * (dprob - jnp.transpose(row_dot, (1, 2, 0))[..., None]) * scale).astype(jnp.bfloat16)
        d_q = jnp.einsum("kgts,skd->tkgd", dscore.astype(jnp.float32), all_keys).astype(jnp.bfloat16)
        d_k = jnp.einsum("kgts,tkgd->skd", dscore.astype(jnp.float32), q_blk)
        d_v = jnp.einsum("kgts,tkgd->skd", weights_bf.astype(jnp.float32), go_blk.astype(jnp.float32))
        partial_value = jnp.stack([d_k, d_v]).reshape(2, 3, TOK_DEV, key_value_heads * HEAD_SIZE)
        return out_bf.reshape(TOK_DEV, key_value_heads * GROUP_FEATURES), d_q.reshape(TOK_DEV, key_value_heads * GROUP_FEATURES), partial_value

    outs, dqs, partials = lax.map(one_block, jnp.arange(n_blocks, dtype=jnp.int32))
    attn_out = outs.reshape(TOKEN_COUNT, key_value_heads * GROUP_FEATURES)
    d_query = dqs.reshape(TOKEN_COUNT, key_value_heads * GROUP_FEATURES)
    total = partials[:, :, 0]
    total = total + jnp.roll(partials[:, :, 1], -1, axis=0)
    total = total + jnp.roll(partials[:, :, 2], -2, axis=0)
    d_keyvalue = jnp.transpose(total, (1, 0, 2, 3)).reshape(2, TOKEN_COUNT, key_value_heads * HEAD_SIZE).astype(jnp.bfloat16)
    grouped = jnp.transpose(attn_out.reshape(TOKEN_COUNT, key_value_heads, GROUP_FEATURES), (1, 0, 2))

    def group_gram(block):
        return jnp.dot(block.T, block, preferred_element_type=jnp.float32)

    gram = lax.map(group_gram, grouped) / (TOKEN_COUNT ** 0.5)
    return attn_out, d_query, d_keyvalue, gram
```

```python
import math

import jax
import jax.numpy as jnp
from jax import lax
from jax.experimental import pallas as pl
from jax.experimental.pallas import tpu as pltpu
from jax.sharding import PartitionSpec as P

NT = (((1,), (1,)), ((), ()))
NN = (((1,), (0,)), ((), ()))
LOWEST = -1e30
VMEM_LIMIT = 48 * 1024 * 1024


def dot(a, b, dims):
    return lax.dot_general(a, b, dims, preferred_element_type=jnp.float32)


def visibility(place_ref, order_ref):
    me = place_ref[0]
    count = order_ref.shape[0]
    mine = order_ref[me]
    out = []
    for step in (1, 2):
        theirs = order_ref[lax.rem(me + count - step, count)]
        out.append(jnp.where(theirs <= mine, 0.0, -LOWEST).astype(jnp.float32))
    return out


def forward_kernel(place_ref, order_ref, q_ref, k0_ref, v0_ref, kv1_ref, kv2_ref, out_ref, out_t_ref, lse_ref):
    tok, dim = k0_ref.shape
    heads = q_ref.shape[1] // dim
    unit = math.log2(math.e) / dim**0.5
    hide = [None] + visibility(place_ref, order_ref)
    keys = [k0_ref[...], kv1_ref[:tok, :], kv2_ref[:tok, :]]
    values_t = [v0_ref[...].T, kv1_ref[tok:, :].T, kv2_ref[tok:, :].T]
    causal = lax.broadcasted_iota(jnp.int32, (tok, tok), 0) <= lax.broadcasted_iota(jnp.int32, (tok, tok), 1)
    for h in range(heads):
        cols = slice(h * dim, (h + 1) * dim)
        qh = q_ref[:, cols]
        scores = [dot(key, qh, NT) for key in keys]
        scores[0] = jnp.where(causal, scores[0], LOWEST)
        top = jnp.max(scores[0], axis=0, keepdims=True) * unit
        for j in (1, 2):
            top = jnp.maximum(top, jnp.max(scores[j], axis=0, keepdims=True) * unit - hide[j])
        total = None
        mixed = None
        for j in range(3):
            base = top if j == 0 else top + hide[j]
            expo = jnp.exp2(scores[j] * unit - base)
            part = jnp.sum(expo, axis=0, keepdims=True)
            total = part if total is None else total + part
            piece = dot(values_t[j], expo.astype(jnp.bfloat16), NN)
            mixed = piece if mixed is None else mixed + piece
        mixed = mixed * (1.0 / total)
        out_t_ref[cols, :] = mixed.astype(jnp.bfloat16)
        out_ref[:, cols] = mixed.T.astype(jnp.bfloat16)
        lse_ref[h:h + 1, :] = top + jnp.log2(total)


def backward_kernel(place_ref, order_ref, q_ref, go_ref, out_ref, lse_ref, k0_ref, v0_ref, kv1_ref, kv2_ref,
                    dq_ref, dkv0_ref, dkv1_ref, dkv2_ref, acc_ref):
    tok, dim = k0_ref.shape
    heads = q_ref.shape[1] // dim
    scale = 1.0 / dim**0.5
    unit = math.log2(math.e) * scale
    hide = [None] + visibility(place_ref, order_ref)
    keys = [k0_ref[...], kv1_ref[:tok, :], kv2_ref[:tok, :]]
    values = [v0_ref[...], kv1_ref[tok:, :], kv2_ref[tok:, :]]
    keys_t = [key.T for key in keys]
    causal = lax.broadcasted_iota(jnp.int32, (tok, tok), 0) <= lax.broadcasted_iota(jnp.int32, (tok, tok), 1)
    for h in range(heads):
        cols = slice(h * dim, (h + 1) * dim)
        qh = q_ref[:, cols]
        gh = go_ref[:, cols]
        lse = lse_ref[h:h + 1, :]
        row_dot = jnp.sum((gh.astype(jnp.float32) * out_ref[:, cols].astype(jnp.float32)).T, axis=0, keepdims=True)
        dq_t = None
        for j in range(3):
            scores = dot(keys[j], qh, NT)
            if j == 0:
                scores = jnp.where(causal, scores, LOWEST)
            base = lse if j == 0 else lse + hide[j]
            weights = jnp.exp2(scores * unit - base)
            dprob = dot(values[j], gh, NT)
            dscore = (weights * (dprob - row_dot)).astype(jnp.bfloat16)
            piece = dot(keys_t[j], dscore, NN)
            dq_t = piece if dq_t is None else dq_t + piece
            dk = dot(dscore, qh, NN)
            dv = dot(weights.astype(jnp.bfloat16), gh, NN)
            if h == 0:
                acc_ref[j, 0] = dk
                acc_ref[j, 1] = dv
            else:
                acc_ref[j, 0] += dk
                acc_ref[j, 1] += dv
        dq_ref[:, cols] = (dq_t * scale).T.astype(jnp.bfloat16)
    for j, ref in enumerate((dkv0_ref, dkv1_ref, dkv2_ref)):
        ref[0] = (acc_ref[j, 0] * scale).astype(ref.dtype)
        ref[1] = acc_ref[j, 1].astype(ref.dtype)


def gram_kernel(place_ref, mine_ref, other_ref, part_ref):
    core = place_ref[1]
    planes, rows, _, unit, tok = mine_ref.shape
    feats = planes * rows * 2 * unit
    left = jnp.concatenate(
        [ref[:, :, core].reshape(planes * rows * unit, tok) for ref in (mine_ref, other_ref)], axis=1
    )
    wide = 2 * rows * unit * 2
    for first in range(0, feats, wide):
        at = first // (2 * rows * unit)
        right = jnp.concatenate([ref[at:at + 2].reshape(wide, tok) for ref in (mine_ref, other_ref)], axis=1)
        got = dot(left, right, NT).astype(jnp.bfloat16)
        for plane in range(planes):
            block = got[plane * rows * unit:(plane + 1) * rows * unit]
            part_ref[:, plane, :, first:first + wide] = block.reshape(rows, unit, wide)


SMEM = pl.BlockSpec(memory_space=pltpu.SMEM)
VMEM = pl.BlockSpec(memory_space=pltpu.VMEM)
PARAMS = pltpu.CompilerParams(vmem_limit_bytes=VMEM_LIMIT)


def forward(place, order, q, k0, v0, kv1, kv2):
    tok, width = q.shape
    heads = width // k0.shape[1]
    return pl.pallas_call(
        forward_kernel,
        out_shape=(jax.ShapeDtypeStruct((tok, width), jnp.bfloat16), jax.ShapeDtypeStruct((width, tok), jnp.bfloat16),
                   jax.ShapeDtypeStruct((heads, tok), jnp.float32)),
        in_specs=[SMEM] * 2 + [VMEM] * 5,
        out_specs=(VMEM,) * 3,
        compiler_params=PARAMS,
        cost_estimate=pl.CostEstimate(flops=4 * tok * width * 3 * tok, bytes_accessed=2000000, transcendentals=0),
        name="attention_forward",
    )(place, order, q, k0, v0, kv1, kv2)


def backward(place, order, q, go, out, lse, k0, v0, kv1, kv2):
    tok, width = q.shape
    dim = k0.shape[1]
    pair = jax.ShapeDtypeStruct((2, tok, dim), jnp.bfloat16)
    return pl.pallas_call(
        backward_kernel,
        out_shape=(jax.ShapeDtypeStruct((tok, width), jnp.bfloat16), jax.ShapeDtypeStruct((2, tok, dim), jnp.float32), pair, pair),
        in_specs=[SMEM] * 2 + [VMEM] * 8,
        out_specs=(VMEM,) * 4,
        scratch_shapes=[pltpu.VMEM((3, 2, tok, dim), jnp.float32)],
        compiler_params=PARAMS,
        cost_estimate=pl.CostEstimate(flops=10 * tok * width * 3 * tok, bytes_accessed=3000000, transcendentals=0),
        name="attention_backward",
    )(place, order, q, go, out, lse, k0, v0, kv1, kv2)


def gram_part(place, mine, other):
    planes, rows, cores, unit, tok = mine.shape
    feats = planes * rows * cores * unit
    return pl.pallas_call(
        gram_kernel,
        out_shape=jax.ShapeDtypeStruct((rows, planes, unit, feats), jnp.bfloat16),
        in_specs=[SMEM] + [VMEM] * 2,
        out_specs=VMEM,
        compiler_params=PARAMS,
        cost_estimate=pl.CostEstimate(flops=2 * feats * feats * tok, bytes_accessed=2000000, transcendentals=0),
        name="gram_part",
    )(place, mine, other)


CORES = 2
ROWS = 4


def shifted(block, distance):
    count = lax.axis_size("seq")
    return lax.ppermute(block, "seq", [(i, (i + distance) % count) for i in range(count)])


def local(query, key_in, value_input, output_gradient, block_order):
    tok, width = query.shape
    count = lax.axis_size("seq")
    planes = count // (CORES * ROWS)
    unit = width // count
    me = lax.axis_index("seq").astype(jnp.int32)
    place = jnp.stack([me, me % CORES])
    held = jnp.concatenate([key_in, value_input])
    kv2 = shifted(held, 2)
    kv1 = shifted(held, 1)
    out, out_t, lse = forward(place, block_order, query, key_in, value_input, kv1, kv2)
    other_t = lax.ppermute(out_t, "seq", [(i, i ^ 1) for i in range(count)])
    split = (planes, ROWS, CORES, unit, tok)
    part = gram_part(place, out_t.reshape(split), other_t.reshape(split))
    row_groups = [[(z * ROWS + y) * CORES + c for y in range(ROWS)] for z in range(planes) for c in range(CORES)]
    plane_groups = [[(z * ROWS + y) * CORES + c for z in range(planes)] for y in range(ROWS) for c in range(CORES)]
    part = lax.all_to_all(part, "seq", 0, 0, axis_index_groups=row_groups, tiled=True)
    d_query, kept, away1, away2 = backward(
        place, block_order, query, output_gradient, out, lse, key_in, value_input, kv1, kv2
    )
    part = jnp.sum(part.astype(jnp.float32), axis=0).astype(jnp.bfloat16)
    back2 = shifted(away2, -2)
    back1 = shifted(away1, -1)
    part = lax.all_to_all(part, "seq", 0, 0, axis_index_groups=plane_groups, tiled=True)
    gram = jnp.sum(part.astype(jnp.float32), axis=0) / (tok * count) ** 0.5
    total = kept + back1.astype(jnp.float32) + back2.astype(jnp.float32)
    return out, d_query, total.astype(jnp.bfloat16), gram[None]


def solution(mesh):
    in_specs = (P("seq", "head"), P("seq", "head"), P("seq", "head"), P("seq", "head"), P())
    out_specs = (P("seq", "head"), P("seq", "head"), P(None, "seq", "head"), P("head", "seq", None))
    return jax.shard_map(local, mesh=mesh, in_specs=in_specs, out_specs=out_specs, check_vma=False)
```

```python
import math

import jax
import jax.numpy as jnp
from jax import lax
from jax.experimental import pallas as pl
from jax.experimental.pallas import tpu as pltpu
from jax.sharding import PartitionSpec as P

NT = (((1,), (1,)), ((), ()))
NN = (((1,), (0,)), ((), ()))
LOWEST = -1e30
VMEM_LIMIT = 16 * 1024 * 1024


def dot(a, b, dims):
    return lax.dot_general(a, b, dims, preferred_element_type=jnp.float32)


def widened(block):
    return jnp.concatenate([block, jnp.ones(block.shape, block.dtype)], 1)


def twice(block):
    return jnp.concatenate([block, block], 1)


def own_kernel(place_ref, order_ref, q_ref, kv0_ref, q_out_ref, mixed_ref, top_ref, facts_ref):
    tok, dim = kv0_ref.shape[0] // 2, kv0_ref.shape[1]
    me = place_ref[0]
    count = order_ref.shape[0]
    mine = order_ref[me]
    for step in (1, 2):
        theirs = order_ref[lax.rem(me + count - step, count)]
        hide = jnp.where(theirs <= mine, 0.0, -LOWEST).astype(jnp.float32)
        facts_ref[step - 1:step, :] = jnp.full((1, dim), hide, jnp.float32)
    facts_ref[2:3, :] = jnp.full((1, dim), place_ref[1].astype(jnp.float32), jnp.float32)
    unit = math.log2(math.e) / dim**0.5
    key = kv0_ref[:tok, :]
    value = widened(kv0_ref[tok:, :])
    causal = lax.broadcasted_iota(jnp.int32, (tok, tok), 1) <= lax.broadcasted_iota(jnp.int32, (tok, tok), 0)
    q_out_ref[...] = q_ref[...]
    for h in range(q_ref.shape[1] // dim):
        scores = jnp.where(causal, dot(q_ref[:, h * dim:(h + 1) * dim], key, NT), LOWEST)
        top = jnp.max(scores, axis=1, keepdims=True) * unit
        expo = jnp.exp2(scores * unit - top)
        mixed_ref[h] = dot(expo.astype(jnp.bfloat16), value, NN)
        top_ref[h] = jnp.broadcast_to(top, (tok, dim))


def forward_kernel(facts_ref, q_ref, mixed_ref, top_ref, kv1_ref, kv2_ref, out_t_ref, lse_ref):
    heads, tok, dim = top_ref.shape
    unit = math.log2(math.e) / dim**0.5
    hide = [facts_ref[j:j + 1, :] for j in range(2)]
    keys = [kv_ref[:tok, :] for kv_ref in (kv1_ref, kv2_ref)]
    values = [widened(kv_ref[tok:, :]) for kv_ref in (kv1_ref, kv2_ref)]
    for h in range(heads):
        cols = slice(h * dim, (h + 1) * dim)
        qh = q_ref[:, cols]
        scores = [dot(qh, key, NT) for key in keys]
        own = top_ref[h]
        top = own
        for j in range(2):
            top = jnp.maximum(top, jnp.max(scores[j], axis=1, keepdims=True) * unit - hide[j])
        mixed = mixed_ref[h] * twice(jnp.exp2(own - top))
        for j in range(2):
            expo = jnp.exp2(scores[j] * unit - twice(top + hide[j]))
            mixed = mixed + dot(expo.astype(jnp.bfloat16), values[j], NN)
        total = mixed[:, dim:]
        out_t_ref[cols, :] = (mixed[:, :dim] / total).T.astype(jnp.bfloat16)
        lse_ref[h:h + 1, :] = (top + jnp.log2(total)).T[:1]


def away_kernel(facts_ref, q_ref, go_ref, out_t_ref, lse_ref, kv1_ref, kv2_ref, away1_ref, away2_ref, dscore_ref,
                row_dot_ref, acc_ref):
    heads, _, tok, _ = dscore_ref.shape
    dim = kv1_ref.shape[1]
    scale = 1.0 / dim**0.5
    unit = math.log2(math.e) * scale
    hide = [twice(facts_ref[j:j + 1, :]) for j in range(2)]
    keys = [kv_ref[:tok, :] for kv_ref in (kv1_ref, kv2_ref)]
    values = [kv_ref[tok:, :] for kv_ref in (kv1_ref, kv2_ref)]
    for h in range(heads):
        cols = slice(h * dim, (h + 1) * dim)
        qh = q_ref[:, cols]
        gh = go_ref[:, cols]
        out_t = out_t_ref[cols, :].astype(jnp.float32)
        row_dot = jnp.sum(gh.astype(jnp.float32).T * out_t, axis=0, keepdims=True)
        row_dot_ref[h:h + 1, :] = row_dot
        for j in range(2):
            weights = jnp.exp2(dot(keys[j], qh, NT) * unit - (lse_ref[h:h + 1, :] + hide[j]))
            dscore = (weights * (dot(values[j], gh, NT) - row_dot)).astype(jnp.bfloat16)
            dscore_ref[h, j] = dscore
            dk = dot(dscore, qh, NN)
            dv = dot(weights.astype(jnp.bfloat16), gh, NN)
            if h > 0:
                dk = acc_ref[j, 0] + dk
                dv = acc_ref[j, 1] + dv
            if h < heads - 1:
                acc_ref[j, 0] = dk
                acc_ref[j, 1] = dv
            else:
                away_ref = (away1_ref, away2_ref)[j]
                away_ref[0] = (dk * scale).astype(away_ref.dtype)
                away_ref[1] = dv.astype(away_ref.dtype)


def backward_kernel(q_ref, go_ref, out_t_ref, lse_ref, row_dot_ref, dscore_ref, kv0_ref, kv1_ref, kv2_ref,
                    out_ref, dq_ref, kept_ref, acc_ref):
    heads, _, tok, _ = dscore_ref.shape
    dim = kv0_ref.shape[1]
    scale = 1.0 / dim**0.5
    unit = math.log2(math.e) * scale
    key = kv0_ref[:tok, :]
    value = kv0_ref[tok:, :]
    keys_t = [kv_ref[:tok, :].T for kv_ref in (kv0_ref, kv1_ref, kv2_ref)]
    causal = lax.broadcasted_iota(jnp.int32, (tok, tok), 0) <= lax.broadcasted_iota(jnp.int32, (tok, tok), 1)
    for h in range(heads):
        cols = slice(h * dim, (h + 1) * dim)
        qh = q_ref[:, cols]
        gh = go_ref[:, cols]
        scores = jnp.where(causal, dot(key, qh, NT), LOWEST)
        weights = jnp.exp2(scores * unit - lse_ref[h:h + 1, :])
        dscore = (weights * (dot(value, gh, NT) - row_dot_ref[h:h + 1, :])).astype(jnp.bfloat16)
        dq_t = dot(keys_t[0], dscore, NN)
        for j in range(2):
            dq_t = dq_t + dot(keys_t[j + 1], dscore_ref[h, j], NN)
        dq_ref[:, cols] = (dq_t * scale).T.astype(jnp.bfloat16)
        out_ref[:, cols] = out_t_ref[cols, :].T
        dk = dot(dscore, qh, NN)
        dv = dot(weights.astype(jnp.bfloat16), gh, NN)
        if h > 0:
            dk = acc_ref[0] + dk
            dv = acc_ref[1] + dv
        if h < heads - 1:
            acc_ref[0] = dk
            acc_ref[1] = dv
        else:
            kept_ref[0] = dk * scale
            kept_ref[1] = dv


def gram_kernel(facts_ref, mine_ref, other_ref, part_hbm, part_ref, sems):
    core = facts_ref[2:3, :1].astype(jnp.bfloat16)
    planes, rows, cores, unit, tok = mine_ref.shape
    chunks = part_ref.shape[0]
    step = planes // chunks
    wide = step * rows * cores * unit
    picked = [ref[:, :, 0] * (1 - core) + ref[:, :, 1] * core for ref in (mine_ref, other_ref)]
    left = jnp.concatenate([block.reshape(planes * rows * unit, tok) for block in picked], axis=1)
    saves = []
    for i in range(chunks):
        right = jnp.concatenate(
            [ref[i * step:(i + 1) * step].reshape(wide, tok) for ref in (mine_ref, other_ref)], axis=1
        )
        got = dot(left, right, NT).astype(jnp.bfloat16)
        for plane in range(planes):
            block = got[plane * rows * unit:(plane + 1) * rows * unit]
            part_ref[i, :, plane] = block.reshape(rows, unit, wide)
        save = pltpu.make_async_copy(part_ref.at[i], part_hbm.at[:, :, :, pl.ds(i * wide, wide)], sems.at[i])
        save.start()
        saves.append(save)
    for save in saves:
        save.wait()


def row_sum_kernel(part_ref, sum_ref):
    total = part_ref[0].astype(jnp.float32)
    for i in range(1, part_ref.shape[0]):
        total = total + part_ref[i].astype(jnp.float32)
    sum_ref[...] = total.astype(sum_ref.dtype)


def key_value_sum_kernel(kept_ref, back1_ref, back2_ref, total_ref):
    total = kept_ref[...] + back1_ref[...].astype(jnp.float32) + back2_ref[...].astype(jnp.float32)
    total_ref[...] = total.astype(total_ref.dtype)


SMEM = pl.BlockSpec(memory_space=pltpu.SMEM)
VMEM = pl.BlockSpec(memory_space=pltpu.VMEM)
HBM = pl.BlockSpec(memory_space=pltpu.HBM)
PARAMS = pltpu.CompilerParams(vmem_limit_bytes=VMEM_LIMIT)


def own_block(place, order, q, kv0):
    tok, width = q.shape
    dim = kv0.shape[1]
    heads = width // dim
    return pl.pallas_call(
        own_kernel,
        out_shape=(jax.ShapeDtypeStruct(q.shape, q.dtype), jax.ShapeDtypeStruct((heads, tok, 2 * dim), jnp.float32),
                   jax.ShapeDtypeStruct((heads, tok, dim), jnp.float32), jax.ShapeDtypeStruct((8, dim), jnp.float32)),
        in_specs=[SMEM] * 2 + [VMEM] * 2,
        out_specs=(VMEM,) * 4,
        compiler_params=PARAMS,
        cost_estimate=pl.CostEstimate(flops=4 * tok * width * tok, bytes_accessed=6000000, transcendentals=0),
        name="own_block",
    )(place, order, q, kv0)


def forward(facts, q, mixed, top, kv1, kv2):
    tok, width = q.shape
    heads = top.shape[0]
    return pl.pallas_call(
        forward_kernel,
        out_shape=(jax.ShapeDtypeStruct((width, tok), jnp.bfloat16), jax.ShapeDtypeStruct((heads, tok), jnp.float32)),
        in_specs=[VMEM] * 6,
        out_specs=(VMEM,) * 2,
        compiler_params=PARAMS,
        cost_estimate=pl.CostEstimate(flops=8 * tok * width * tok, bytes_accessed=2000000, transcendentals=0),
        name="attention_forward",
    )(facts, q, mixed, top, kv1, kv2)


def away_gradients(facts, q, go, out_t, lse, kv1, kv2):
    tok, width = q.shape
    dim = kv1.shape[1]
    heads = width // dim
    pair = jax.ShapeDtypeStruct((2, tok, dim), jnp.bfloat16)
    return pl.pallas_call(
        away_kernel,
        out_shape=(pair, pair, jax.ShapeDtypeStruct((heads, 2, tok, tok), jnp.bfloat16),
                   jax.ShapeDtypeStruct((heads, tok), jnp.float32)),
        in_specs=[VMEM] * 7,
        out_specs=(VMEM,) * 4,
        scratch_shapes=[pltpu.VMEM((2, 2, tok, dim), jnp.float32)],
        compiler_params=PARAMS,
        cost_estimate=pl.CostEstimate(flops=16 * tok * width * tok, bytes_accessed=3000000, transcendentals=0),
        name="away_gradients",
    )(facts, q, go, out_t, lse, kv1, kv2)


def backward(q, go, out_t, lse, row_dot, dscore, kv0, kv1, kv2):
    tok, width = q.shape
    dim = kv0.shape[1]
    full = jax.ShapeDtypeStruct((tok, width), jnp.bfloat16)
    return pl.pallas_call(
        backward_kernel,
        out_shape=(full, full, jax.ShapeDtypeStruct((2, tok, dim), jnp.float32)),
        in_specs=[VMEM] * 9,
        out_specs=(VMEM,) * 3,
        scratch_shapes=[pltpu.VMEM((2, tok, dim), jnp.float32)],
        compiler_params=PARAMS,
        cost_estimate=pl.CostEstimate(flops=14 * tok * width * tok, bytes_accessed=3000000, transcendentals=0),
        name="attention_backward",
    )(q, go, out_t, lse, row_dot, dscore, kv0, kv1, kv2)


def gram_part(facts, mine, other):
    planes, rows, cores, unit, tok = mine.shape
    feats = planes * rows * cores * unit
    chunks = 4
    return pl.pallas_call(
        gram_kernel,
        out_shape=jax.ShapeDtypeStruct((rows, planes, unit, feats), jnp.bfloat16),
        in_specs=[VMEM] * 3,
        out_specs=HBM,
        scratch_shapes=[pltpu.VMEM((chunks, rows, planes, unit, feats // chunks), jnp.bfloat16),
                        pltpu.SemaphoreType.DMA((chunks,))],
        compiler_params=PARAMS,
        cost_estimate=pl.CostEstimate(flops=2 * feats * feats * tok, bytes_accessed=2000000, transcendentals=0),
        name="gram_part",
    )(facts, mine, other)


def row_sum(part):
    return pl.pallas_call(
        row_sum_kernel,
        out_shape=jax.ShapeDtypeStruct(part.shape[1:], part.dtype),
        in_specs=[VMEM],
        out_specs=VMEM,
        compiler_params=PARAMS,
        cost_estimate=pl.CostEstimate(flops=part.size, bytes_accessed=part.size * 2, transcendentals=0),
        name="row_sum",
    )(part)


def key_value_sum(kept, back1, back2):
    return pl.pallas_call(
        key_value_sum_kernel,
        out_shape=jax.ShapeDtypeStruct(kept.shape, jnp.bfloat16),
        in_specs=[VMEM] * 3,
        out_specs=VMEM,
        compiler_params=PARAMS,
        cost_estimate=pl.CostEstimate(flops=20 * 10**9, bytes_accessed=50 * 10**6, transcendentals=0),
        name="key_value_sum",
    )(kept, back1, back2)


CORES = 2
ROWS = 4


def shifted(block, distance):
    count = lax.axis_size("seq")
    return lax.ppermute(block, "seq", [(i, (i + distance) % count) for i in range(count)])


def local(query, key_in, value_input, output_gradient, block_order):
    tok, width = query.shape
    count = lax.axis_size("seq")
    planes = count // (CORES * ROWS)
    unit = width // count
    me = lax.axis_index("seq").astype(jnp.int32)
    place = jnp.stack([me, me % CORES])
    kv0 = jnp.stack([key_in, value_input]).reshape(2 * tok, -1)
    kv2 = shifted(kv0, 2)
    kv1 = shifted(kv0, 1)
    q_near, mixed, top, facts = own_block(place, block_order, query, kv0)
    out_t, lse = forward(facts, q_near, mixed, top, kv1, kv2)
    other_t = lax.ppermute(out_t, "seq", [(i, i ^ 1) for i in range(count)])
    split = (planes, ROWS, CORES, unit, tok)
    part = gram_part(facts, out_t.reshape(split), other_t.reshape(split))
    row_groups = [[(z * ROWS + y) * CORES + c for y in range(ROWS)] for z in range(planes) for c in range(CORES)]
    plane_groups = [[(z * ROWS + y) * CORES + c for z in range(planes)] for y in range(ROWS) for c in range(CORES)]
    part, lse = lax.optimization_barrier((part, lse))
    part = lax.all_to_all(part, "seq", 0, 0, axis_index_groups=row_groups, tiled=True)
    away1, away2, dscore, row_dot = away_gradients(facts, q_near, output_gradient, out_t, lse, kv1, kv2)
    back2 = shifted(away2, -2)
    back1 = shifted(away1, -1)
    out, d_query, kept = backward(q_near, output_gradient, out_t, lse, row_dot, dscore, kv0, kv1, kv2)
    part = row_sum(part)
    part, row_dot = lax.optimization_barrier((part, row_dot))
    part = lax.all_to_all(part, "seq", 0, 0, axis_index_groups=plane_groups, tiled=True)
    gram = jnp.sum(part.astype(jnp.float32), axis=0) / (tok * count) ** 0.5
    return out, d_query, key_value_sum(kept, back1, back2), gram[None]


def solution(mesh):
    in_specs = (P("seq", "head"), P("seq", "head"), P("seq", "head"), P("seq", "head"), P())
    out_specs = (P("seq", "head"), P("seq", "head"), P(None, "seq", "head"), P("head", "seq", None))
    return jax.shard_map(local, mesh=mesh, in_specs=in_specs, out_specs=out_specs, check_vma=False)
```

```python
import math

import jax
import jax.numpy as jnp
from jax import lax
from jax.experimental import pallas as pl
from jax.experimental.pallas import tpu as pltpu
from jax.sharding import PartitionSpec as P

NT = (((1,), (1,)), ((), ()))
NN = (((1,), (0,)), ((), ()))
LOWEST = -1e30
VMEM_LIMIT = 16 * 1024 * 1024


def dot(a, b, dims):
    return lax.dot_general(a, b, dims, preferred_element_type=jnp.float32)


def widened(block):
    return jnp.concatenate([block, jnp.ones(block.shape, block.dtype)], 1)


def twice(block):
    return jnp.concatenate([block, block], 1)


def own_kernel(place_ref, order_ref, q_ref, kv0_ref, q_out_ref, mixed_ref, top_ref, facts_ref):
    tok, dim = kv0_ref.shape[0] // 2, kv0_ref.shape[1]
    me = place_ref[0]
    count = order_ref.shape[0]
    mine = order_ref[me]
    for step in (1, 2):
        theirs = order_ref[lax.rem(me + count - step, count)]
        hide = jnp.where(theirs <= mine, 0.0, -LOWEST).astype(jnp.float32)
        facts_ref[step - 1:step, :] = jnp.full((1, dim), hide, jnp.float32)
    facts_ref[2:3, :] = jnp.full((1, dim), place_ref[1].astype(jnp.float32), jnp.float32)
    unit = math.log2(math.e) / dim**0.5
    key = kv0_ref[:tok, :]
    value = widened(kv0_ref[tok:, :])
    causal = lax.broadcasted_iota(jnp.int32, (tok, tok), 1) <= lax.broadcasted_iota(jnp.int32, (tok, tok), 0)
    q_out_ref[...] = q_ref[...]
    for h in range(q_ref.shape[1] // dim):
        scores = jnp.where(causal, dot(q_ref[:, h * dim:(h + 1) * dim], key, NT), LOWEST)
        top = jnp.max(scores, axis=1, keepdims=True) * unit
        expo = jnp.exp2(scores * unit - top)
        mixed_ref[h] = dot(expo.astype(jnp.bfloat16), value, NN)
        top_ref[h] = jnp.broadcast_to(top, (tok, dim))


def forward_kernel(facts_ref, q_ref, mixed_ref, top_ref, kv1_ref, kv2_ref, out_t_ref, lse_ref):
    heads, tok, dim = top_ref.shape
    unit = math.log2(math.e) / dim**0.5
    hide = [facts_ref[j:j + 1, :] for j in range(2)]
    keys = [kv_ref[:tok, :] for kv_ref in (kv1_ref, kv2_ref)]
    values = [widened(kv_ref[tok:, :]) for kv_ref in (kv1_ref, kv2_ref)]
    for h in range(heads):
        cols = slice(h * dim, (h + 1) * dim)
        qh = q_ref[:, cols]
        scores = [dot(qh, key, NT) for key in keys]
        own = top_ref[h]
        top = own
        for j in range(2):
            top = jnp.maximum(top, jnp.max(scores[j], axis=1, keepdims=True) * unit - hide[j])
        mixed = mixed_ref[h] * twice(jnp.exp2(own - top))
        for j in range(2):
            expo = jnp.exp2(scores[j] * unit - twice(top + hide[j]))
            mixed = mixed + dot(expo.astype(jnp.bfloat16), values[j], NN)
        total = mixed[:, dim:]
        out_t_ref[cols, :] = (mixed[:, :dim] / total).T.astype(jnp.bfloat16)
        lse_ref[h:h + 1, :] = (top + jnp.log2(total)).T[:1]


def away_kernel(facts_ref, q_ref, go_ref, out_t_ref, lse_ref, kv1_ref, kv2_ref, away1_ref, away2_ref, out_hbm, dscore_ref,
                row_dot_ref, acc_ref, out_ref, sems):
    heads, _, tok, _ = dscore_ref.shape
    dim = kv1_ref.shape[1]
    scale = 1.0 / dim**0.5
    unit = math.log2(math.e) * scale
    hide = [twice(facts_ref[j:j + 1, :]) for j in range(2)]
    saves = [pltpu.make_async_copy(out_ref.at[h], out_hbm.at[:, pl.ds(h * dim, dim)], sems.at[h]) for h in range(heads)]
    keys = [kv_ref[:tok, :] for kv_ref in (kv1_ref, kv2_ref)]
    values = [kv_ref[tok:, :] for kv_ref in (kv1_ref, kv2_ref)]
    for h in range(heads):
        cols = slice(h * dim, (h + 1) * dim)
        qh = q_ref[:, cols]
        gh = go_ref[:, cols]
        out_t = out_t_ref[cols, :].astype(jnp.float32)
        row_dot = jnp.sum(gh.astype(jnp.float32).T * out_t, axis=0, keepdims=True)
        row_dot_ref[h:h + 1, :] = row_dot
        out_ref[h] = out_t.T.astype(jnp.bfloat16)
        saves[h].start()
        for j in range(2):
            weights = jnp.exp2(dot(keys[j], qh, NT) * unit - (lse_ref[h:h + 1, :] + hide[j]))
            dscore = (weights * (dot(values[j], gh, NT) - row_dot)).astype(jnp.bfloat16)
            dscore_ref[h, j] = dscore
            dk = dot(dscore, qh, NN)
            dv = dot(weights.astype(jnp.bfloat16), gh, NN)
            if h > 0:
                dk = acc_ref[j, 0] + dk
                dv = acc_ref[j, 1] + dv
            if h < heads - 1:
                acc_ref[j, 0] = dk
                acc_ref[j, 1] = dv
            else:
                away_ref = (away1_ref, away2_ref)[j]
                away_ref[0] = (dk * scale).astype(away_ref.dtype)
                away_ref[1] = dv.astype(away_ref.dtype)
    for save in saves:
        save.wait()


def backward_kernel(q_ref, go_ref, lse_ref, row_dot_ref, dscore_ref, kv0_ref, kv1_ref, kv2_ref, after_ref, dq_ref, kept_ref, acc_ref):
    heads, _, tok, _ = dscore_ref.shape
    dim = kv0_ref.shape[1]
    scale = 1.0 / dim**0.5
    unit = math.log2(math.e) * scale
    key = kv0_ref[:tok, :]
    value = kv0_ref[tok:, :]
    keys_t = [kv_ref[:tok, :].T for kv_ref in (kv0_ref, kv1_ref, kv2_ref)]
    causal = lax.broadcasted_iota(jnp.int32, (tok, tok), 0) <= lax.broadcasted_iota(jnp.int32, (tok, tok), 1)
    for h in range(heads):
        cols = slice(h * dim, (h + 1) * dim)
        qh = q_ref[:, cols]
        gh = go_ref[:, cols]
        scores = jnp.where(causal, dot(key, qh, NT), LOWEST)
        weights = jnp.exp2(scores * unit - lse_ref[h:h + 1, :])
        dscore = (weights * (dot(value, gh, NT) - row_dot_ref[h:h + 1, :])).astype(jnp.bfloat16)
        dq_t = dot(keys_t[0], dscore, NN)
        for j in range(2):
            dq_t = dq_t + dot(keys_t[j + 1], dscore_ref[h, j], NN)
        dq_ref[:, cols] = (dq_t * scale).T.astype(jnp.bfloat16)
        dk = dot(dscore, qh, NN)
        dv = dot(weights.astype(jnp.bfloat16), gh, NN)
        if h > 0:
            dk = acc_ref[0] + dk
            dv = acc_ref[1] + dv
        if h < heads - 1:
            acc_ref[0] = dk
            acc_ref[1] = dv
        else:
            kept_ref[0] = dk * scale
            kept_ref[1] = dv


def gram_kernel(facts_ref, mine_ref, other_ref, part_hbm, part_ref, sems):
    core = facts_ref[2:3, :1].astype(jnp.bfloat16)
    planes, rows, cores, unit, tok = mine_ref.shape
    chunks = part_ref.shape[0]
    step = planes // chunks
    wide = step * rows * cores * unit
    picked = [ref[:, :, 0] * (1 - core) + ref[:, :, 1] * core for ref in (mine_ref, other_ref)]
    left = jnp.concatenate([block.reshape(planes * rows * unit, tok) for block in picked], axis=1)
    saves = []
    for i in range(chunks):
        right = jnp.concatenate(
            [ref[i * step:(i + 1) * step].reshape(wide, tok) for ref in (mine_ref, other_ref)], axis=1
        )
        got = dot(left, right, NT).astype(jnp.bfloat16)
        for plane in range(planes):
            block = got[plane * rows * unit:(plane + 1) * rows * unit]
            first = (plane % 2) * rows
            part_ref[i, first:first + rows, plane // 2] = block.reshape(rows, unit, wide)
        save = pltpu.make_async_copy(part_ref.at[i], part_hbm.at[:, :, :, pl.ds(i * wide, wide)], sems.at[i])
        save.start()
        saves.append(save)
    for save in saves:
        save.wait()


def row_sum_kernel(part_ref, sum_ref):
    total = part_ref[0].astype(jnp.float32)
    for i in range(1, part_ref.shape[0]):
        total = total + part_ref[i].astype(jnp.float32)
    sum_ref[...] = total.astype(sum_ref.dtype)


def key_value_sum_kernel(kept_ref, back1_ref, back2_ref, total_ref):
    total = kept_ref[...] + back1_ref[...].astype(jnp.float32) + back2_ref[...].astype(jnp.float32)
    total_ref[...] = total.astype(total_ref.dtype)


SMEM = pl.BlockSpec(memory_space=pltpu.SMEM)
VMEM = pl.BlockSpec(memory_space=pltpu.VMEM)
HBM = pl.BlockSpec(memory_space=pltpu.HBM)
PARAMS = pltpu.CompilerParams(vmem_limit_bytes=VMEM_LIMIT)


def own_block(place, order, q, kv0):
    tok, width = q.shape
    dim = kv0.shape[1]
    heads = width // dim
    return pl.pallas_call(
        own_kernel,
        out_shape=(jax.ShapeDtypeStruct(q.shape, q.dtype), jax.ShapeDtypeStruct((heads, tok, 2 * dim), jnp.float32),
                   jax.ShapeDtypeStruct((heads, tok, dim), jnp.float32), jax.ShapeDtypeStruct((8, dim), jnp.float32)),
        in_specs=[SMEM] * 2 + [VMEM] * 2,
        out_specs=(VMEM,) * 4,
        compiler_params=PARAMS,
        cost_estimate=pl.CostEstimate(flops=4 * tok * width * tok, bytes_accessed=6000000, transcendentals=0),
        name="own_block",
    )(place, order, q, kv0)


def forward(facts, q, mixed, top, kv1, kv2):
    tok, width = q.shape
    heads = top.shape[0]
    return pl.pallas_call(
        forward_kernel,
        out_shape=(jax.ShapeDtypeStruct((width, tok), jnp.bfloat16), jax.ShapeDtypeStruct((heads, tok), jnp.float32)),
        in_specs=[VMEM] * 6,
        out_specs=(VMEM,) * 2,
        compiler_params=PARAMS,
        cost_estimate=pl.CostEstimate(flops=8 * tok * width * tok, bytes_accessed=2000000, transcendentals=0),
        name="attention_forward",
    )(facts, q, mixed, top, kv1, kv2)


def away_gradients(facts, q, go, out_t, lse, kv1, kv2):
    tok, width = q.shape
    dim = kv1.shape[1]
    heads = width // dim
    pair = jax.ShapeDtypeStruct((2, tok, dim), jnp.bfloat16)
    return pl.pallas_call(
        away_kernel,
        out_shape=(pair, pair, jax.ShapeDtypeStruct((tok, width), jnp.bfloat16),
                   jax.ShapeDtypeStruct((heads, 2, tok, tok), jnp.bfloat16), jax.ShapeDtypeStruct((heads, tok), jnp.float32)),
        in_specs=[VMEM] * 7,
        out_specs=(VMEM, VMEM, HBM, VMEM, VMEM),
        scratch_shapes=[pltpu.VMEM((2, 2, tok, dim), jnp.float32), pltpu.VMEM((heads, tok, dim), jnp.bfloat16),
                        pltpu.SemaphoreType.DMA((heads,))],
        compiler_params=PARAMS,
        cost_estimate=pl.CostEstimate(flops=16 * tok * width * tok, bytes_accessed=3000000, transcendentals=0),
        name="away_gradients",
    )(facts, q, go, out_t, lse, kv1, kv2)


def backward(q, go, lse, row_dot, dscore, kv0, kv1, kv2, after):
    tok, width = q.shape
    dim = kv0.shape[1]
    full = jax.ShapeDtypeStruct((tok, width), jnp.bfloat16)
    return pl.pallas_call(
        backward_kernel,
        out_shape=(full, jax.ShapeDtypeStruct((2, tok, dim), jnp.float32)),
        in_specs=[VMEM] * 8 + [HBM],
        out_specs=(VMEM,) * 2,
        scratch_shapes=[pltpu.VMEM((2, tok, dim), jnp.float32)],
        compiler_params=PARAMS,
        cost_estimate=pl.CostEstimate(flops=14 * tok * width * tok, bytes_accessed=3000000, transcendentals=0),
        name="attention_backward",
    )(q, go, lse, row_dot, dscore, kv0, kv1, kv2, after)


def gram_part(facts, mine, other):
    planes, rows, cores, unit, tok = mine.shape
    feats = planes * rows * cores * unit
    chunks = 4
    return pl.pallas_call(
        gram_kernel,
        out_shape=jax.ShapeDtypeStruct((2 * rows, planes // 2, unit, feats), jnp.bfloat16),
        in_specs=[VMEM] * 3,
        out_specs=HBM,
        scratch_shapes=[pltpu.VMEM((chunks, 2 * rows, planes // 2, unit, feats // chunks), jnp.bfloat16),
                        pltpu.SemaphoreType.DMA((chunks,))],
        compiler_params=PARAMS,
        cost_estimate=pl.CostEstimate(flops=2 * feats * feats * tok, bytes_accessed=2000000, transcendentals=0),
        name="gram_part",
    )(facts, mine, other)


def row_sum(part):
    return pl.pallas_call(
        row_sum_kernel,
        out_shape=jax.ShapeDtypeStruct(part.shape[1:], part.dtype),
        in_specs=[VMEM],
        out_specs=VMEM,
        compiler_params=PARAMS,
        cost_estimate=pl.CostEstimate(flops=part.size, bytes_accessed=part.size * 2, transcendentals=0),
        name="row_sum",
    )(part)


def key_value_sum(kept, back1, back2):
    return pl.pallas_call(
        key_value_sum_kernel,
        out_shape=jax.ShapeDtypeStruct(kept.shape, jnp.bfloat16),
        in_specs=[VMEM] * 3,
        out_specs=VMEM,
        compiler_params=PARAMS,
        cost_estimate=pl.CostEstimate(flops=20 * 10**9, bytes_accessed=50 * 10**6, transcendentals=0),
        name="key_value_sum",
    )(kept, back1, back2)


CORES = 2
ROWS = 4


def shifted(block, distance):
    count = lax.axis_size("seq")
    return lax.ppermute(block, "seq", [(i, (i + distance) % count) for i in range(count)])


def local(query, key_in, value_input, output_gradient, block_order):
    tok, width = query.shape
    count = lax.axis_size("seq")
    planes = count // (CORES * ROWS)
    unit = width // count
    me = lax.axis_index("seq").astype(jnp.int32)
    place = jnp.stack([me, me % CORES])
    kv0 = jnp.stack([key_in, value_input]).reshape(2 * tok, -1)
    kv2 = shifted(kv0, 2)
    kv1 = shifted(kv0, 1)
    q_near, mixed, top, facts = own_block(place, block_order, query, kv0)
    out_t, lse = forward(facts, q_near, mixed, top, kv1, kv2)
    other_t = lax.ppermute(out_t, "seq", [(i, i ^ 1) for i in range(count)])
    split = (planes, ROWS, CORES, unit, tok)
    part = gram_part(facts, out_t.reshape(split), other_t.reshape(split))
    seat = lambda z, y, c: (z * ROWS + y) * CORES + c
    near_groups = [
        [seat(2 * half + side, y, c) for side in range(2) for y in range(ROWS)]
        for half in range(planes // 2) for c in range(CORES)
    ]
    far_groups = [
        [seat(2 * half + side, y, c) for half in range(planes // 2)]
        for side in range(2) for y in range(ROWS) for c in range(CORES)
    ]
    part, lse = lax.optimization_barrier((part, lse))
    part = lax.all_to_all(part, "seq", 0, 0, axis_index_groups=near_groups, tiled=True)
    away1, away2, out, dscore, row_dot = away_gradients(facts, q_near, output_gradient, out_t, lse, kv1, kv2)
    back2 = shifted(away2, -2)
    back1 = shifted(away1, -1)
    part = row_sum(part)
    d_query, kept = backward(q_near, output_gradient, lse, row_dot, dscore, kv0, kv1, kv2, part)
    part = lax.all_to_all(part, "seq", 0, 0, axis_index_groups=far_groups, tiled=True)
    gram = jnp.sum(part.astype(jnp.float32), axis=0) / (tok * count) ** 0.5
    return out, d_query, key_value_sum(kept, back1, back2), gram[None]


def solution(mesh):
    in_specs = (P("seq", "head"), P("seq", "head"), P("seq", "head"), P("seq", "head"), P())
    out_specs = (P("seq", "head"), P("seq", "head"), P(None, "seq", "head"), P("head", "seq", None))
    return jax.shard_map(local, mesh=mesh, in_specs=in_specs, out_specs=out_specs, check_vma=False)
```

```python
import math

import jax
import jax.numpy as jnp
from jax import lax
from jax.experimental import pallas as pl
from jax.experimental.pallas import tpu as pltpu
from jax.sharding import PartitionSpec as P

NT = (((1,), (1,)), ((), ()))
NN = (((1,), (0,)), ((), ()))
LOWEST = -1e30
VMEM_LIMIT = 16 * 1024 * 1024


def dot(a, b, dims):
    return lax.dot_general(a, b, dims, preferred_element_type=jnp.float32)


def widened(block):
    return jnp.concatenate([block, jnp.ones(block.shape, block.dtype)], 1)


def twice(block):
    return jnp.concatenate([block, block], 1)


def own_kernel(place_ref, order_ref, q_ref, kv0_ref, q_out_ref, mixed_ref, top_ref, facts_ref):
    tok, dim = kv0_ref.shape[0] // 2, kv0_ref.shape[1]
    me = place_ref[0]
    count = order_ref.shape[0]
    mine = order_ref[me]
    for step in (1, 2):
        theirs = order_ref[lax.rem(me + count - step, count)]
        hide = jnp.where(theirs <= mine, 0.0, -LOWEST).astype(jnp.float32)
        facts_ref[step - 1:step, :] = jnp.full((1, dim), hide, jnp.float32)
    facts_ref[2:3, :] = jnp.full((1, dim), place_ref[1].astype(jnp.float32), jnp.float32)
    unit = math.log2(math.e) / dim**0.5
    key = kv0_ref[:tok, :]
    value = widened(kv0_ref[tok:, :])
    causal = lax.broadcasted_iota(jnp.int32, (tok, tok), 1) <= lax.broadcasted_iota(jnp.int32, (tok, tok), 0)
    q_out_ref[...] = q_ref[...]
    for h in range(q_ref.shape[1] // dim):
        scores = jnp.where(causal, dot(q_ref[:, h * dim:(h + 1) * dim], key, NT), LOWEST)
        top = jnp.max(scores, axis=1, keepdims=True) * unit
        expo = jnp.exp2(scores * unit - top)
        mixed_ref[h] = dot(expo.astype(jnp.bfloat16), value, NN)
        top_ref[h] = jnp.broadcast_to(top, (tok, dim))


def forward_kernel(facts_ref, q_ref, mixed_ref, top_ref, kv1_ref, kv2_ref, out_t_ref, lse_ref):
    heads, tok, dim = top_ref.shape
    unit = math.log2(math.e) / dim**0.5
    hide = [facts_ref[j:j + 1, :] for j in range(2)]
    keys = [kv_ref[:tok, :] for kv_ref in (kv1_ref, kv2_ref)]
    values = [widened(kv_ref[tok:, :]) for kv_ref in (kv1_ref, kv2_ref)]
    for h in range(heads):
        cols = slice(h * dim, (h + 1) * dim)
        qh = q_ref[:, cols]
        scores = [dot(qh, key, NT) for key in keys]
        own = top_ref[h]
        top = own
        for j in range(2):
            top = jnp.maximum(top, jnp.max(scores[j], axis=1, keepdims=True) * unit - hide[j])
        mixed = mixed_ref[h] * twice(jnp.exp2(own - top))
        for j in range(2):
            expo = jnp.exp2(scores[j] * unit - twice(top + hide[j]))
            mixed = mixed + dot(expo.astype(jnp.bfloat16), values[j], NN)
        total = mixed[:, dim:]
        out_t_ref[cols, :] = (mixed[:, :dim] / total).T.astype(jnp.bfloat16)
        lse_ref[h:h + 1, :] = (top + jnp.log2(total)).T[:1]


def away_kernel(facts_ref, q_ref, go_ref, out_t_ref, lse_ref, kv1_ref, kv2_ref, away1_ref, away2_ref, out_hbm, dscore_ref,
                row_dot_ref, acc_ref, out_ref, sems):
    heads, _, tok, _ = dscore_ref.shape
    dim = kv1_ref.shape[1]
    scale = 1.0 / dim**0.5
    unit = math.log2(math.e) * scale
    hide = [twice(facts_ref[j:j + 1, :]) for j in range(2)]
    saves = [pltpu.make_async_copy(out_ref.at[h], out_hbm.at[:, pl.ds(h * dim, dim)], sems.at[h]) for h in range(heads)]
    keys = [kv_ref[:tok, :] for kv_ref in (kv1_ref, kv2_ref)]
    values = [kv_ref[tok:, :] for kv_ref in (kv1_ref, kv2_ref)]
    for h in range(heads):
        cols = slice(h * dim, (h + 1) * dim)
        qh = q_ref[:, cols]
        gh = go_ref[:, cols]
        out_t = out_t_ref[cols, :].astype(jnp.float32)
        row_dot = jnp.sum(gh.astype(jnp.float32).T * out_t, axis=0, keepdims=True)
        row_dot_ref[h:h + 1, :] = row_dot
        out_ref[h] = out_t.T.astype(jnp.bfloat16)
        saves[h].start()
        for j in range(2):
            weights = jnp.exp2(dot(keys[j], qh, NT) * unit - (lse_ref[h:h + 1, :] + hide[j]))
            dscore = (weights * (dot(values[j], gh, NT) - row_dot)).astype(jnp.bfloat16)
            dscore_ref[h, j] = dscore
            dk = dot(dscore, qh, NN)
            dv = dot(weights.astype(jnp.bfloat16), gh, NN)
            if h > 0:
                dk = acc_ref[j, 0] + dk
                dv = acc_ref[j, 1] + dv
            if h < heads - 1:
                acc_ref[j, 0] = dk
                acc_ref[j, 1] = dv
            else:
                away_ref = (away1_ref, away2_ref)[j]
                away_ref[0] = (dk * scale).astype(away_ref.dtype)
                away_ref[1] = dv.astype(away_ref.dtype)
    for save in saves:
        save.wait()


def backward_kernel(q_ref, go_ref, lse_ref, row_dot_ref, dscore_ref, kv0_ref, kv1_ref, kv2_ref, after_ref, dq_ref, kept_ref, acc_ref):
    heads, _, tok, _ = dscore_ref.shape
    dim = kv0_ref.shape[1]
    scale = 1.0 / dim**0.5
    unit = math.log2(math.e) * scale
    key = kv0_ref[:tok, :]
    value = kv0_ref[tok:, :]
    keys_t = [kv_ref[:tok, :].T for kv_ref in (kv0_ref, kv1_ref, kv2_ref)]
    causal = lax.broadcasted_iota(jnp.int32, (tok, tok), 0) <= lax.broadcasted_iota(jnp.int32, (tok, tok), 1)
    for h in range(heads):
        cols = slice(h * dim, (h + 1) * dim)
        qh = q_ref[:, cols]
        gh = go_ref[:, cols]
        scores = jnp.where(causal, dot(key, qh, NT), LOWEST)
        weights = jnp.exp2(scores * unit - lse_ref[h:h + 1, :])
        dscore = (weights * (dot(value, gh, NT) - row_dot_ref[h:h + 1, :])).astype(jnp.bfloat16)
        dq_t = dot(keys_t[0], dscore, NN)
        for j in range(2):
            dq_t = dq_t + dot(keys_t[j + 1], dscore_ref[h, j], NN)
        dq_ref[:, cols] = (dq_t * scale).T.astype(jnp.bfloat16)
        dk = dot(dscore, qh, NN)
        dv = dot(weights.astype(jnp.bfloat16), gh, NN)
        if h > 0:
            dk = acc_ref[0] + dk
            dv = acc_ref[1] + dv
        if h < heads - 1:
            acc_ref[0] = dk
            acc_ref[1] = dv
        else:
            kept_ref[0] = dk * scale
            kept_ref[1] = dv


def gram_kernel(facts_ref, both_ref, part_hbm, part_ref, sems):
    core = facts_ref[2:3, :1].astype(jnp.bfloat16)
    _, planes, rows, cores, unit, tok = both_ref.shape
    chunks = part_ref.shape[0]
    step = planes // chunks
    wide = step * rows * cores * unit
    picked = [both_ref[i, :, :, 0] * (1 - core) + both_ref[i, :, :, 1] * core for i in range(2)]
    left = jnp.concatenate([block.reshape(planes * rows * unit, tok) for block in picked], axis=1)
    saves = []
    for i in range(chunks):
        right = jnp.concatenate(
            [both_ref[j, i * step:(i + 1) * step].reshape(wide, tok) for j in range(2)], axis=1
        )
        got = dot(left, right, NT).astype(jnp.bfloat16)
        for plane in range(planes):
            block = got[plane * rows * unit:(plane + 1) * rows * unit]
            first = (plane % 2) * rows
            part_ref[i, first:first + rows, plane // 2] = block.reshape(rows, unit, wide)
        save = pltpu.make_async_copy(part_ref.at[i], part_hbm.at[:, :, :, pl.ds(i * wide, wide)], sems.at[i])
        save.start()
        saves.append(save)
    for save in saves:
        save.wait()


def row_sum_kernel(part_ref, sum_ref):
    total = part_ref[0].astype(jnp.float32)
    for i in range(1, part_ref.shape[0]):
        total = total + part_ref[i].astype(jnp.float32)
    sum_ref[...] = total.astype(sum_ref.dtype)


def key_value_sum_kernel(kept_ref, back1_ref, back2_ref, total_ref):
    total = kept_ref[...] + back1_ref[...].astype(jnp.float32) + back2_ref[...].astype(jnp.float32)
    total_ref[...] = total.astype(total_ref.dtype)


SMEM = pl.BlockSpec(memory_space=pltpu.SMEM)
VMEM = pl.BlockSpec(memory_space=pltpu.VMEM)
HBM = pl.BlockSpec(memory_space=pltpu.HBM)
PARAMS = pltpu.CompilerParams(vmem_limit_bytes=VMEM_LIMIT)


def own_block(place, order, q, kv0):
    tok, width = q.shape
    dim = kv0.shape[1]
    heads = width // dim
    return pl.pallas_call(
        own_kernel,
        out_shape=(jax.ShapeDtypeStruct(q.shape, q.dtype), jax.ShapeDtypeStruct((heads, tok, 2 * dim), jnp.float32),
                   jax.ShapeDtypeStruct((heads, tok, dim), jnp.float32), jax.ShapeDtypeStruct((8, dim), jnp.float32)),
        in_specs=[SMEM] * 2 + [VMEM] * 2,
        out_specs=(VMEM,) * 4,
        compiler_params=PARAMS,
        cost_estimate=pl.CostEstimate(flops=4 * tok * width * tok, bytes_accessed=6000000, transcendentals=0),
        name="own_block",
    )(place, order, q, kv0)


def forward(facts, q, mixed, top, kv1, kv2):
    tok, width = q.shape
    heads = top.shape[0]
    return pl.pallas_call(
        forward_kernel,
        out_shape=(jax.ShapeDtypeStruct((width, tok), jnp.bfloat16), jax.ShapeDtypeStruct((heads, tok), jnp.float32)),
        in_specs=[VMEM] * 6,
        out_specs=(VMEM,) * 2,
        compiler_params=PARAMS,
        cost_estimate=pl.CostEstimate(flops=8 * tok * width * tok, bytes_accessed=2000000, transcendentals=0),
        name="attention_forward",
    )(facts, q, mixed, top, kv1, kv2)


def away_gradients(facts, q, go, out_t, lse, kv1, kv2):
    tok, width = q.shape
    dim = kv1.shape[1]
    heads = width // dim
    pair = jax.ShapeDtypeStruct((2, tok, dim), jnp.bfloat16)
    return pl.pallas_call(
        away_kernel,
        out_shape=(pair, pair, jax.ShapeDtypeStruct((tok, width), jnp.bfloat16),
                   jax.ShapeDtypeStruct((heads, 2, tok, tok), jnp.bfloat16), jax.ShapeDtypeStruct((heads, tok), jnp.float32)),
        in_specs=[VMEM] * 7,
        out_specs=(VMEM, VMEM, HBM, VMEM, VMEM),
        scratch_shapes=[pltpu.VMEM((2, 2, tok, dim), jnp.float32), pltpu.VMEM((heads, tok, dim), jnp.bfloat16),
                        pltpu.SemaphoreType.DMA((heads,))],
        compiler_params=PARAMS,
        cost_estimate=pl.CostEstimate(flops=16 * tok * width * tok, bytes_accessed=3000000, transcendentals=0),
        name="away_gradients",
    )(facts, q, go, out_t, lse, kv1, kv2)


def backward(q, go, lse, row_dot, dscore, kv0, kv1, kv2, after):
    tok, width = q.shape
    dim = kv0.shape[1]
    full = jax.ShapeDtypeStruct((tok, width), jnp.bfloat16)
    return pl.pallas_call(
        backward_kernel,
        out_shape=(full, jax.ShapeDtypeStruct((2, tok, dim), jnp.float32)),
        in_specs=[VMEM] * 8 + [HBM],
        out_specs=(VMEM,) * 2,
        scratch_shapes=[pltpu.VMEM((2, tok, dim), jnp.float32)],
        compiler_params=PARAMS,
        cost_estimate=pl.CostEstimate(flops=14 * tok * width * tok, bytes_accessed=3000000, transcendentals=0),
        name="attention_backward",
    )(q, go, lse, row_dot, dscore, kv0, kv1, kv2, after)


def gram_part(facts, both):
    _, planes, rows, cores, unit, tok = both.shape
    feats = planes * rows * cores * unit
    chunks = 2
    return pl.pallas_call(
        gram_kernel,
        out_shape=jax.ShapeDtypeStruct((2 * rows, planes // 2, unit, feats), jnp.bfloat16),
        in_specs=[VMEM] * 2,
        out_specs=HBM,
        scratch_shapes=[pltpu.VMEM((chunks, 2 * rows, planes // 2, unit, feats // chunks), jnp.bfloat16),
                        pltpu.SemaphoreType.DMA((chunks,))],
        compiler_params=PARAMS,
        cost_estimate=pl.CostEstimate(flops=2 * feats * feats * tok, bytes_accessed=2000000, transcendentals=0),
        name="gram_part",
    )(facts, both)


def row_sum(part):
    return pl.pallas_call(
        row_sum_kernel,
        out_shape=jax.ShapeDtypeStruct(part.shape[1:], part.dtype),
        in_specs=[VMEM],
        out_specs=VMEM,
        compiler_params=PARAMS,
        cost_estimate=pl.CostEstimate(flops=part.size, bytes_accessed=part.size * 2, transcendentals=0),
        name="row_sum",
    )(part)


def key_value_sum(kept, back1, back2):
    return pl.pallas_call(
        key_value_sum_kernel,
        out_shape=jax.ShapeDtypeStruct(kept.shape, jnp.bfloat16),
        in_specs=[VMEM] * 3,
        out_specs=VMEM,
        compiler_params=PARAMS,
        cost_estimate=pl.CostEstimate(flops=20 * 10**9, bytes_accessed=50 * 10**6, transcendentals=0),
        name="key_value_sum",
    )(kept, back1, back2)


CORES = 2
ROWS = 4


def shifted(block, distance):
    count = lax.axis_size("seq")
    return lax.ppermute(block, "seq", [(i, (i + distance) % count) for i in range(count)])


def local(query, key_in, value_input, output_gradient, block_order):
    tok, width = query.shape
    count = lax.axis_size("seq")
    planes = count // (CORES * ROWS)
    unit = width // count
    me = lax.axis_index("seq").astype(jnp.int32)
    place = jnp.stack([me, me % CORES])
    kv0 = jnp.stack([key_in, value_input]).reshape(2 * tok, -1)
    kv2 = shifted(kv0, 2)
    kv1 = shifted(kv0, 1)
    q_near, mixed, top, facts = own_block(place, block_order, query, kv0)
    out_t, lse = forward(facts, q_near, mixed, top, kv1, kv2)
    pairs = [[i, i + 1] for i in range(0, count, CORES)]
    both = lax.all_gather(out_t, "seq", axis_index_groups=pairs)
    part = gram_part(facts, both.reshape(CORES, planes, ROWS, CORES, unit, tok))
    seat = lambda z, y, c: (z * ROWS + y) * CORES + c
    near_groups = [
        [seat(2 * half + side, y, c) for side in range(2) for y in range(ROWS)]
        for half in range(planes // 2) for c in range(CORES)
    ]
    far_groups = [
        [seat(2 * half + side, y, c) for half in range(planes // 2)]
        for side in range(2) for y in range(ROWS) for c in range(CORES)
    ]
    part, lse = lax.optimization_barrier((part, lse))
    part = lax.all_to_all(part, "seq", 0, 0, axis_index_groups=near_groups, tiled=True)
    away1, away2, out, dscore, row_dot = away_gradients(facts, q_near, output_gradient, out_t, lse, kv1, kv2)
    back2 = shifted(away2, -2)
    back1 = shifted(away1, -1)
    part = row_sum(part)
    d_query, kept = backward(q_near, output_gradient, lse, row_dot, dscore, kv0, kv1, kv2, part)
    part = lax.all_to_all(part, "seq", 0, 0, axis_index_groups=far_groups, tiled=True)
    gram = jnp.sum(part.astype(jnp.float32), axis=0) / (tok * count) ** 0.5
    return out, d_query, key_value_sum(kept, back1, back2), gram[None]


def solution(mesh):
    in_specs = (P("seq", "head"), P("seq", "head"), P("seq", "head"), P("seq", "head"), P())
    out_specs = (P("seq", "head"), P("seq", "head"), P(None, "seq", "head"), P("head", "seq", None))
    return jax.shard_map(local, mesh=mesh, in_specs=in_specs, out_specs=out_specs, check_vma=False)
```

```python
import math

import jax
import jax.numpy as jnp
from jax import lax
from jax.experimental import pallas as pl
from jax.experimental.pallas import tpu as pltpu
from jax.sharding import PartitionSpec as P

NT = (((1,), (1,)), ((), ()))
NN = (((1,), (0,)), ((), ()))
LOWEST = -1e30
VMEM_LIMIT = 16 * 1024 * 1024


def dot(a, b, dims):
    return lax.dot_general(a, b, dims, preferred_element_type=jnp.float32)


def widened(block):
    return jnp.concatenate([block, jnp.ones(block.shape, block.dtype)], 1)


def twice(block):
    return jnp.concatenate([block, block], 1)


def own_kernel(place_ref, order_ref, q_ref, kv0_ref, q_out_ref, mixed_ref, top_ref, facts_ref):
    tok, dim = kv0_ref.shape[0] // 2, kv0_ref.shape[1]
    me = place_ref[0]
    count = order_ref.shape[0]
    mine = order_ref[me]
    for step in (1, 2):
        theirs = order_ref[lax.rem(me + count - step, count)]
        hide = jnp.where(theirs <= mine, 0.0, -LOWEST).astype(jnp.float32)
        facts_ref[step - 1:step, :] = jnp.full((1, dim), hide, jnp.float32)
    facts_ref[2:3, :] = jnp.full((1, dim), place_ref[1].astype(jnp.float32), jnp.float32)
    unit = math.log2(math.e) / dim**0.5
    key = kv0_ref[:tok, :]
    value = widened(kv0_ref[tok:, :])
    causal = lax.broadcasted_iota(jnp.int32, (tok, tok), 1) <= lax.broadcasted_iota(jnp.int32, (tok, tok), 0)
    q_out_ref[...] = q_ref[...]
    for h in range(q_ref.shape[1] // dim):
        scores = jnp.where(causal, dot(q_ref[:, h * dim:(h + 1) * dim], key, NT), LOWEST)
        top = jnp.max(scores, axis=1, keepdims=True) * unit
        expo = jnp.exp2(scores * unit - top)
        mixed_ref[h] = dot(expo.astype(jnp.bfloat16), value, NN)
        top_ref[h] = jnp.broadcast_to(top, (tok, dim))


def forward_kernel(facts_ref, q_ref, mixed_ref, top_ref, pair_ref, even2_ref, out_t_ref, lse_ref, kv1_ref, kv2_ref):
    heads, tok, dim = top_ref.shape
    core = facts_ref[2:3, :1].astype(jnp.bfloat16)
    kv1_ref[...] = pair_ref[0] * core + pair_ref[1] * (1 - core)
    kv2_ref[...] = pair_ref[1] * core + even2_ref[...] * (1 - core)
    unit = math.log2(math.e) / dim**0.5
    hide = [facts_ref[j:j + 1, :] for j in range(2)]
    keys = [kv_ref[:tok, :] for kv_ref in (kv1_ref, kv2_ref)]
    values = [widened(kv_ref[tok:, :]) for kv_ref in (kv1_ref, kv2_ref)]
    for h in range(heads):
        cols = slice(h * dim, (h + 1) * dim)
        qh = q_ref[:, cols]
        scores = [dot(qh, key, NT) for key in keys]
        own = top_ref[h]
        top = own
        for j in range(2):
            top = jnp.maximum(top, jnp.max(scores[j], axis=1, keepdims=True) * unit - hide[j])
        mixed = mixed_ref[h] * twice(jnp.exp2(own - top))
        for j in range(2):
            expo = jnp.exp2(scores[j] * unit - twice(top + hide[j]))
            mixed = mixed + dot(expo.astype(jnp.bfloat16), values[j], NN)
        total = mixed[:, dim:]
        out_t_ref[cols, :] = (mixed[:, :dim] / total).T.astype(jnp.bfloat16)
        lse_ref[h:h + 1, :] = (top + jnp.log2(total)).T[:1]


def away_kernel(facts_ref, q_ref, go_ref, out_t_ref, lse_ref, kv1_ref, kv2_ref, away1_ref, away2_ref, out_hbm, dscore_ref,
                row_dot_ref, acc_ref, out_ref, sems):
    heads, _, tok, _ = dscore_ref.shape
    dim = kv1_ref.shape[1]
    scale = 1.0 / dim**0.5
    unit = math.log2(math.e) * scale
    hide = [twice(facts_ref[j:j + 1, :]) for j in range(2)]
    saves = [pltpu.make_async_copy(out_ref.at[h], out_hbm.at[:, pl.ds(h * dim, dim)], sems.at[h]) for h in range(heads)]
    keys = [kv_ref[:tok, :] for kv_ref in (kv1_ref, kv2_ref)]
    values = [kv_ref[tok:, :] for kv_ref in (kv1_ref, kv2_ref)]
    for h in range(heads):
        cols = slice(h * dim, (h + 1) * dim)
        qh = q_ref[:, cols]
        gh = go_ref[:, cols]
        out_t = out_t_ref[cols, :].astype(jnp.float32)
        row_dot = jnp.sum(gh.astype(jnp.float32).T * out_t, axis=0, keepdims=True)
        row_dot_ref[h:h + 1, :] = row_dot
        out_ref[h] = out_t.T.astype(jnp.bfloat16)
        saves[h].start()
        for j in range(2):
            weights = jnp.exp2(dot(keys[j], qh, NT) * unit - (lse_ref[h:h + 1, :] + hide[j]))
            dscore = (weights * (dot(values[j], gh, NT) - row_dot)).astype(jnp.bfloat16)
            dscore_ref[h, j] = dscore
            dk = dot(dscore, qh, NN)
            dv = dot(weights.astype(jnp.bfloat16), gh, NN)
            if h > 0:
                dk = acc_ref[j, 0] + dk
                dv = acc_ref[j, 1] + dv
            if h < heads - 1:
                acc_ref[j, 0] = dk
                acc_ref[j, 1] = dv
            else:
                away_ref = (away1_ref, away2_ref)[j]
                away_ref[0] = (dk * scale).astype(away_ref.dtype)
                away_ref[1] = dv.astype(away_ref.dtype)
    for save in saves:
        save.wait()


def backward_kernel(q_ref, go_ref, lse_ref, row_dot_ref, dscore_ref, kv0_ref, kv1_ref, kv2_ref, after_ref, dq_ref, kept_ref, acc_ref):
    heads, _, tok, _ = dscore_ref.shape
    dim = kv0_ref.shape[1]
    scale = 1.0 / dim**0.5
    unit = math.log2(math.e) * scale
    key = kv0_ref[:tok, :]
    value = kv0_ref[tok:, :]
    keys_t = [kv_ref[:tok, :].T for kv_ref in (kv0_ref, kv1_ref, kv2_ref)]
    causal = lax.broadcasted_iota(jnp.int32, (tok, tok), 0) <= lax.broadcasted_iota(jnp.int32, (tok, tok), 1)
    for h in range(heads):
        cols = slice(h * dim, (h + 1) * dim)
        qh = q_ref[:, cols]
        gh = go_ref[:, cols]
        scores = jnp.where(causal, dot(key, qh, NT), LOWEST)
        weights = jnp.exp2(scores * unit - lse_ref[h:h + 1, :])
        dscore = (weights * (dot(value, gh, NT) - row_dot_ref[h:h + 1, :])).astype(jnp.bfloat16)
        dq_t = dot(keys_t[0], dscore, NN)
        for j in range(2):
            dq_t = dq_t + dot(keys_t[j + 1], dscore_ref[h, j], NN)
        dq_ref[:, cols] = (dq_t * scale).T.astype(jnp.bfloat16)
        dk = dot(dscore, qh, NN)
        dv = dot(weights.astype(jnp.bfloat16), gh, NN)
        if h > 0:
            dk = acc_ref[0] + dk
            dv = acc_ref[1] + dv
        if h < heads - 1:
            acc_ref[0] = dk
            acc_ref[1] = dv
        else:
            kept_ref[0] = dk * scale
            kept_ref[1] = dv


def gram_kernel(facts_ref, mine_ref, other_ref, part_hbm, part_ref, sems):
    core = facts_ref[2:3, :1].astype(jnp.bfloat16)
    planes, rows, cores, unit, tok = mine_ref.shape
    chunks = part_ref.shape[0]
    step = planes // chunks
    wide = step * rows * cores * unit
    picked = [ref[:, :, 0] * (1 - core) + ref[:, :, 1] * core for ref in (mine_ref, other_ref)]
    left = jnp.concatenate([block.reshape(planes * rows * unit, tok) for block in picked], axis=1)
    saves = []
    for i in range(chunks):
        right = jnp.concatenate(
            [ref[i * step:(i + 1) * step].reshape(wide, tok) for ref in (mine_ref, other_ref)], axis=1
        )
        got = dot(left, right, NT).astype(jnp.bfloat16)
        for plane in range(planes):
            block = got[plane * rows * unit:(plane + 1) * rows * unit]
            first = (plane % 2) * rows
            part_ref[i, first:first + rows, plane // 2] = block.reshape(rows, unit, wide)
        save = pltpu.make_async_copy(part_ref.at[i], part_hbm.at[:, :, :, pl.ds(i * wide, wide)], sems.at[i])
        save.start()
        saves.append(save)
    for save in saves:
        save.wait()


def row_sum_kernel(part_ref, sum_ref):
    total = part_ref[0].astype(jnp.float32)
    for i in range(1, part_ref.shape[0]):
        total = total + part_ref[i].astype(jnp.float32)
    sum_ref[...] = total.astype(sum_ref.dtype)


def key_value_sum_kernel(kept_ref, back1_ref, back2_ref, total_ref):
    total = kept_ref[...] + back1_ref[...].astype(jnp.float32) + back2_ref[...].astype(jnp.float32)
    total_ref[...] = total.astype(total_ref.dtype)


SMEM = pl.BlockSpec(memory_space=pltpu.SMEM)
VMEM = pl.BlockSpec(memory_space=pltpu.VMEM)
HBM = pl.BlockSpec(memory_space=pltpu.HBM)
PARAMS = pltpu.CompilerParams(vmem_limit_bytes=VMEM_LIMIT)


def own_block(place, order, q, kv0):
    tok, width = q.shape
    dim = kv0.shape[1]
    heads = width // dim
    return pl.pallas_call(
        own_kernel,
        out_shape=(jax.ShapeDtypeStruct(q.shape, q.dtype), jax.ShapeDtypeStruct((heads, tok, 2 * dim), jnp.float32),
                   jax.ShapeDtypeStruct((heads, tok, dim), jnp.float32), jax.ShapeDtypeStruct((8, dim), jnp.float32)),
        in_specs=[SMEM] * 2 + [VMEM] * 2,
        out_specs=(VMEM,) * 4,
        compiler_params=PARAMS,
        cost_estimate=pl.CostEstimate(flops=4 * tok * width * tok, bytes_accessed=6000000, transcendentals=0),
        name="own_block",
    )(place, order, q, kv0)


def forward(facts, q, mixed, top, pair, even2):
    tok, width = q.shape
    heads = top.shape[0]
    return pl.pallas_call(
        forward_kernel,
        out_shape=(jax.ShapeDtypeStruct((width, tok), jnp.bfloat16), jax.ShapeDtypeStruct((heads, tok), jnp.float32),
                   jax.ShapeDtypeStruct(even2.shape, even2.dtype), jax.ShapeDtypeStruct(even2.shape, even2.dtype)),
        in_specs=[VMEM] * 6,
        out_specs=(VMEM,) * 4,
        compiler_params=PARAMS,
        cost_estimate=pl.CostEstimate(flops=8 * tok * width * tok, bytes_accessed=2000000, transcendentals=0),
        name="attention_forward",
    )(facts, q, mixed, top, pair, even2)


def away_gradients(facts, q, go, out_t, lse, kv1, kv2):
    tok, width = q.shape
    dim = kv1.shape[1]
    heads = width // dim
    pair = jax.ShapeDtypeStruct((2, tok, dim), jnp.bfloat16)
    return pl.pallas_call(
        away_kernel,
        out_shape=(pair, pair, jax.ShapeDtypeStruct((tok, width), jnp.bfloat16),
                   jax.ShapeDtypeStruct((heads, 2, tok, tok), jnp.bfloat16), jax.ShapeDtypeStruct((heads, tok), jnp.float32)),
        in_specs=[VMEM] * 7,
        out_specs=(VMEM, VMEM, HBM, VMEM, VMEM),
        scratch_shapes=[pltpu.VMEM((2, 2, tok, dim), jnp.float32), pltpu.VMEM((heads, tok, dim), jnp.bfloat16),
                        pltpu.SemaphoreType.DMA((heads,))],
        compiler_params=PARAMS,
        cost_estimate=pl.CostEstimate(flops=16 * tok * width * tok, bytes_accessed=3000000, transcendentals=0),
        name="away_gradients",
    )(facts, q, go, out_t, lse, kv1, kv2)


def backward(q, go, lse, row_dot, dscore, kv0, kv1, kv2, after):
    tok, width = q.shape
    dim = kv0.shape[1]
    full = jax.ShapeDtypeStruct((tok, width), jnp.bfloat16)
    return pl.pallas_call(
        backward_kernel,
        out_shape=(full, jax.ShapeDtypeStruct((2, tok, dim), jnp.float32)),
        in_specs=[VMEM] * 8 + [HBM],
        out_specs=(VMEM,) * 2,
        scratch_shapes=[pltpu.VMEM((2, tok, dim), jnp.float32)],
        compiler_params=PARAMS,
        cost_estimate=pl.CostEstimate(flops=14 * tok * width * tok, bytes_accessed=3000000, transcendentals=0),
        name="attention_backward",
    )(q, go, lse, row_dot, dscore, kv0, kv1, kv2, after)


def gram_part(facts, mine, other):
    planes, rows, cores, unit, tok = mine.shape
    feats = planes * rows * cores * unit
    chunks = 4
    return pl.pallas_call(
        gram_kernel,
        out_shape=jax.ShapeDtypeStruct((2 * rows, planes // 2, unit, feats), jnp.bfloat16),
        in_specs=[VMEM] * 3,
        out_specs=HBM,
        scratch_shapes=[pltpu.VMEM((chunks, 2 * rows, planes // 2, unit, feats // chunks), jnp.bfloat16),
                        pltpu.SemaphoreType.DMA((chunks,))],
        compiler_params=PARAMS,
        cost_estimate=pl.CostEstimate(flops=2 * feats * feats * tok, bytes_accessed=2000000, transcendentals=0),
        name="gram_part",
    )(facts, mine, other)


def row_sum(part):
    return pl.pallas_call(
        row_sum_kernel,
        out_shape=jax.ShapeDtypeStruct(part.shape[1:], part.dtype),
        in_specs=[VMEM],
        out_specs=VMEM,
        compiler_params=PARAMS,
        cost_estimate=pl.CostEstimate(flops=part.size, bytes_accessed=part.size * 2, transcendentals=0),
        name="row_sum",
    )(part)


def key_value_sum(kept, back1, back2):
    return pl.pallas_call(
        key_value_sum_kernel,
        out_shape=jax.ShapeDtypeStruct(kept.shape, jnp.bfloat16),
        in_specs=[VMEM] * 3,
        out_specs=VMEM,
        compiler_params=PARAMS,
        cost_estimate=pl.CostEstimate(flops=20 * 10**9, bytes_accessed=50 * 10**6, transcendentals=0),
        name="key_value_sum",
    )(kept, back1, back2)


CORES = 2
ROWS = 4


def shifted(block, distance, cores=range(CORES)):
    count = lax.axis_size("seq")
    return lax.ppermute(block, "seq", [(i, (i + distance) % count) for i in range(count) if i % CORES in cores])


def local(query, key_in, value_input, output_gradient, block_order):
    tok, width = query.shape
    count = lax.axis_size("seq")
    planes = count // (CORES * ROWS)
    unit = width // count
    me = lax.axis_index("seq").astype(jnp.int32)
    place = jnp.stack([me, me % CORES])
    kv0 = jnp.stack([key_in, value_input]).reshape(2 * tok, -1)
    odd2 = shifted(kv0, 2, (1,))
    even2 = shifted(kv0, 2, (0,))
    q_near, mixed, top, facts = own_block(place, block_order, query, kv0)
    core = me % CORES
    pairs = [[i, i + 1] for i in range(0, count, CORES)]
    pair = lax.all_gather(jnp.where(core == 0, kv0, odd2), "seq", axis_index_groups=pairs)
    out_t, lse, kv1, kv2 = forward(facts, q_near, mixed, top, pair, even2)
    other_t = lax.ppermute(out_t, "seq", [(i, i ^ 1) for i in range(count)])
    split = (planes, ROWS, CORES, unit, tok)
    part = gram_part(facts, out_t.reshape(split), other_t.reshape(split))
    seat = lambda z, y, c: (z * ROWS + y) * CORES + c
    near_groups = [
        [seat(2 * half + side, y, c) for side in range(2) for y in range(ROWS)]
        for half in range(planes // 2) for c in range(CORES)
    ]
    far_groups = [
        [seat(2 * half + side, y, c) for half in range(planes // 2)]
        for side in range(2) for y in range(ROWS) for c in range(CORES)
    ]
    part, lse = lax.optimization_barrier((part, lse))
    part = lax.all_to_all(part, "seq", 0, 0, axis_index_groups=near_groups, tiled=True)
    away1, away2, out, dscore, row_dot = away_gradients(facts, q_near, output_gradient, out_t, lse, kv1, kv2)
    pair = lax.all_gather(away1, "seq", axis_index_groups=pairs)
    other = jnp.where(core == 0, pair[1], pair[0])
    sent = jnp.where(core == 0, away2, away2 + other)
    back1 = jnp.where(core == 0, other, jnp.zeros_like(other))
    back2 = shifted(sent, -2)
    part = row_sum(part)
    d_query, kept = backward(q_near, output_gradient, lse, row_dot, dscore, kv0, kv1, kv2, part)
    part = lax.all_to_all(part, "seq", 0, 0, axis_index_groups=far_groups, tiled=True)
    gram = jnp.sum(part.astype(jnp.float32), axis=0) / (tok * count) ** 0.5
    return out, d_query, key_value_sum(kept, back1, back2), gram[None]


def solution(mesh):
    in_specs = (P("seq", "head"), P("seq", "head"), P("seq", "head"), P("seq", "head"), P())
    out_specs = (P("seq", "head"), P("seq", "head"), P(None, "seq", "head"), P("head", "seq", None))
    return jax.shard_map(local, mesh=mesh, in_specs=in_specs, out_specs=out_specs, check_vma=False)
```

```python
import math

import jax
import jax.numpy as jnp
from jax import lax
from jax.experimental import pallas as pl
from jax.experimental.pallas import tpu as pltpu
from jax.sharding import PartitionSpec as P

NT = (((1,), (1,)), ((), ()))
NN = (((1,), (0,)), ((), ()))
LOWEST = -1e30
VMEM_LIMIT = 16 * 1024 * 1024


def dot(a, b, dims):
    return lax.dot_general(a, b, dims, preferred_element_type=jnp.float32)


def widened(block):
    return jnp.concatenate([block, jnp.ones(block.shape, block.dtype)], 1)


def twice(block):
    return jnp.concatenate([block, block], 1)


def own_kernel(place_ref, order_ref, q_ref, kv0_ref, q_out_ref, mixed_ref, top_ref, facts_ref):
    tok, dim = kv0_ref.shape[0] // 2, kv0_ref.shape[1]
    me = place_ref[0]
    count = order_ref.shape[0]
    mine = order_ref[me]
    for step in (1, 2):
        theirs = order_ref[lax.rem(me + count - step, count)]
        hide = jnp.where(theirs <= mine, 0.0, -LOWEST).astype(jnp.float32)
        facts_ref[step - 1:step, :] = jnp.full((1, dim), hide, jnp.float32)
    facts_ref[2:3, :] = jnp.full((1, dim), place_ref[1].astype(jnp.float32), jnp.float32)
    unit = math.log2(math.e) / dim**0.5
    key = kv0_ref[:tok, :]
    value = widened(kv0_ref[tok:, :])
    causal = lax.broadcasted_iota(jnp.int32, (tok, tok), 1) <= lax.broadcasted_iota(jnp.int32, (tok, tok), 0)
    q_out_ref[...] = q_ref[...]
    for h in range(q_ref.shape[1] // dim):
        scores = jnp.where(causal, dot(q_ref[:, h * dim:(h + 1) * dim], key, NT), LOWEST)
        top = jnp.max(scores, axis=1, keepdims=True) * unit
        expo = jnp.exp2(scores * unit - top)
        mixed_ref[h] = dot(expo.astype(jnp.bfloat16), value, NN)
        top_ref[h] = jnp.broadcast_to(top, (tok, dim))


def forward_kernel(facts_ref, even2_ref, q_ref, mixed_ref, top_ref, pair_ref, out_t_ref, lse_ref, kv1_ref, kv2_ref):
    heads, tok, dim = top_ref.shape
    core = facts_ref[2:3, :1].astype(jnp.bfloat16)
    kv1_ref[...] = pair_ref[0] * core + pair_ref[1] * (1 - core)
    kv2_ref[...] = pair_ref[1] * core + even2_ref[...] * (1 - core)
    unit = math.log2(math.e) / dim**0.5
    hide = [facts_ref[j:j + 1, :] for j in range(2)]
    keys = [kv_ref[:tok, :] for kv_ref in (kv1_ref, kv2_ref)]
    values = [widened(kv_ref[tok:, :]) for kv_ref in (kv1_ref, kv2_ref)]
    for h in range(heads):
        cols = slice(h * dim, (h + 1) * dim)
        qh = q_ref[:, cols]
        scores = [dot(qh, key, NT) for key in keys]
        own = top_ref[h]
        top = own
        for j in range(2):
            top = jnp.maximum(top, jnp.max(scores[j], axis=1, keepdims=True) * unit - hide[j])
        mixed = mixed_ref[h] * twice(jnp.exp2(own - top))
        for j in range(2):
            expo = jnp.exp2(scores[j] * unit - twice(top + hide[j]))
            mixed = mixed + dot(expo.astype(jnp.bfloat16), values[j], NN)
        total = mixed[:, dim:]
        out_t_ref[cols, :] = (mixed[:, :dim] / total).T.astype(jnp.bfloat16)
        lse_ref[h:h + 1, :] = (top + jnp.log2(total)).T[:1]


def away_kernel(facts_ref, q_ref, go_ref, out_t_ref, lse_ref, kv1_ref, kv2_ref, away1_ref, away2_ref, out_hbm, dscore_ref,
                row_dot_ref, acc_ref, out_ref, sems):
    heads, _, tok, _ = dscore_ref.shape
    dim = kv1_ref.shape[1]
    scale = 1.0 / dim**0.5
    unit = math.log2(math.e) * scale
    hide = [twice(facts_ref[j:j + 1, :]) for j in range(2)]
    saves = [pltpu.make_async_copy(out_ref.at[h], out_hbm.at[:, pl.ds(h * dim, dim)], sems.at[h]) for h in range(heads)]
    keys = [kv_ref[:tok, :] for kv_ref in (kv1_ref, kv2_ref)]
    values = [kv_ref[tok:, :] for kv_ref in (kv1_ref, kv2_ref)]
    for h in range(heads):
        cols = slice(h * dim, (h + 1) * dim)
        qh = q_ref[:, cols]
        gh = go_ref[:, cols]
        out_t = out_t_ref[cols, :].astype(jnp.float32)
        row_dot = jnp.sum(gh.astype(jnp.float32).T * out_t, axis=0, keepdims=True)
        row_dot_ref[h:h + 1, :] = row_dot
        out_ref[h] = out_t.T.astype(jnp.bfloat16)
        saves[h].start()
        for j in range(2):
            weights = jnp.exp2(dot(keys[j], qh, NT) * unit - (lse_ref[h:h + 1, :] + hide[j]))
            dscore = (weights * (dot(values[j], gh, NT) - row_dot)).astype(jnp.bfloat16)
            dscore_ref[h, j] = dscore
            dk = dot(dscore, qh, NN)
            dv = dot(weights.astype(jnp.bfloat16), gh, NN)
            if h > 0:
                dk = acc_ref[j, 0] + dk
                dv = acc_ref[j, 1] + dv
            if h < heads - 1:
                acc_ref[j, 0] = dk
                acc_ref[j, 1] = dv
            else:
                away_ref = (away1_ref, away2_ref)[j]
                away_ref[0] = (dk * scale).astype(away_ref.dtype)
                away_ref[1] = dv.astype(away_ref.dtype)
    for save in saves:
        save.wait()


def backward_kernel(q_ref, go_ref, lse_ref, row_dot_ref, dscore_ref, kv0_ref, kv1_ref, kv2_ref, after_ref, dq_ref, kept_ref, acc_ref):
    heads, _, tok, _ = dscore_ref.shape
    dim = kv0_ref.shape[1]
    scale = 1.0 / dim**0.5
    unit = math.log2(math.e) * scale
    key = kv0_ref[:tok, :]
    value = kv0_ref[tok:, :]
    keys_t = [kv_ref[:tok, :].T for kv_ref in (kv0_ref, kv1_ref, kv2_ref)]
    causal = lax.broadcasted_iota(jnp.int32, (tok, tok), 0) <= lax.broadcasted_iota(jnp.int32, (tok, tok), 1)
    for h in range(heads):
        cols = slice(h * dim, (h + 1) * dim)
        qh = q_ref[:, cols]
        gh = go_ref[:, cols]
        scores = jnp.where(causal, dot(key, qh, NT), LOWEST)
        weights = jnp.exp2(scores * unit - lse_ref[h:h + 1, :])
        dscore = (weights * (dot(value, gh, NT) - row_dot_ref[h:h + 1, :])).astype(jnp.bfloat16)
        dq_t = dot(keys_t[0], dscore, NN)
        for j in range(2):
            dq_t = dq_t + dot(keys_t[j + 1], dscore_ref[h, j], NN)
        dq_ref[:, cols] = (dq_t * scale).T.astype(jnp.bfloat16)
        dk = dot(dscore, qh, NN)
        dv = dot(weights.astype(jnp.bfloat16), gh, NN)
        if h > 0:
            dk = acc_ref[0] + dk
            dv = acc_ref[1] + dv
        if h < heads - 1:
            acc_ref[0] = dk
            acc_ref[1] = dv
        else:
            kept_ref[0] = dk * scale
            kept_ref[1] = dv


def gram_kernel(facts_ref, mine_ref, other_ref, part_hbm, part_ref, sems):
    core = facts_ref[2:3, :1].astype(jnp.bfloat16)
    planes, rows, cores, unit, tok = mine_ref.shape
    chunks = part_ref.shape[0]
    step = planes // chunks
    wide = step * rows * cores * unit
    picked = [ref[:, :, 0] * (1 - core) + ref[:, :, 1] * core for ref in (mine_ref, other_ref)]
    left = jnp.concatenate([block.reshape(planes * rows * unit, tok) for block in picked], axis=1)
    saves = []
    for i in range(chunks):
        right = jnp.concatenate(
            [ref[i * step:(i + 1) * step].reshape(wide, tok) for ref in (mine_ref, other_ref)], axis=1
        )
        got = dot(left, right, NT).astype(jnp.bfloat16)
        for plane in range(planes):
            block = got[plane * rows * unit:(plane + 1) * rows * unit]
            first = (plane % 2) * rows
            part_ref[i, first:first + rows, plane // 2] = block.reshape(rows, unit, wide)
        save = pltpu.make_async_copy(part_ref.at[i], part_hbm.at[:, :, :, pl.ds(i * wide, wide)], sems.at[i])
        save.start()
        saves.append(save)
    for save in saves:
        save.wait()


def row_sum_kernel(part_ref, sum_ref):
    total = part_ref[0].astype(jnp.float32)
    for i in range(1, part_ref.shape[0]):
        total = total + part_ref[i].astype(jnp.float32)
    sum_ref[...] = total.astype(sum_ref.dtype)


def key_value_sum_kernel(kept_ref, back1_ref, back2_ref, total_ref):
    total = kept_ref[...] + back1_ref[...].astype(jnp.float32) + back2_ref[...].astype(jnp.float32)
    total_ref[...] = total.astype(total_ref.dtype)


SMEM = pl.BlockSpec(memory_space=pltpu.SMEM)
VMEM = pl.BlockSpec(memory_space=pltpu.VMEM)
HBM = pl.BlockSpec(memory_space=pltpu.HBM)
PARAMS = pltpu.CompilerParams(vmem_limit_bytes=VMEM_LIMIT)


def own_block(place, order, q, kv0):
    tok, width = q.shape
    dim = kv0.shape[1]
    heads = width // dim
    return pl.pallas_call(
        own_kernel,
        out_shape=(jax.ShapeDtypeStruct(q.shape, q.dtype), jax.ShapeDtypeStruct((heads, tok, 2 * dim), jnp.float32),
                   jax.ShapeDtypeStruct((heads, tok, dim), jnp.float32), jax.ShapeDtypeStruct((8, dim), jnp.float32)),
        in_specs=[SMEM] * 2 + [VMEM] * 2,
        out_specs=(VMEM,) * 4,
        compiler_params=PARAMS,
        cost_estimate=pl.CostEstimate(flops=4 * tok * width * tok, bytes_accessed=6000000, transcendentals=0),
        name="own_block",
    )(place, order, q, kv0)


def forward(facts, even2, q, mixed, top, pair):
    tok, width = q.shape
    heads = top.shape[0]
    return pl.pallas_call(
        forward_kernel,
        out_shape=(jax.ShapeDtypeStruct((width, tok), jnp.bfloat16), jax.ShapeDtypeStruct((heads, tok), jnp.float32),
                   jax.ShapeDtypeStruct(even2.shape, even2.dtype), jax.ShapeDtypeStruct(even2.shape, even2.dtype)),
        in_specs=[VMEM] * 6,
        out_specs=(VMEM,) * 4,
        compiler_params=PARAMS,
        cost_estimate=pl.CostEstimate(flops=8 * tok * width * tok, bytes_accessed=2000000, transcendentals=0),
        name="attention_forward",
    )(facts, even2, q, mixed, top, pair)


def away_gradients(facts, q, go, out_t, lse, kv1, kv2):
    tok, width = q.shape
    dim = kv1.shape[1]
    heads = width // dim
    pair = jax.ShapeDtypeStruct((2, tok, dim), jnp.bfloat16)
    return pl.pallas_call(
        away_kernel,
        out_shape=(pair, pair, jax.ShapeDtypeStruct((tok, width), jnp.bfloat16),
                   jax.ShapeDtypeStruct((heads, 2, tok, tok), jnp.bfloat16), jax.ShapeDtypeStruct((heads, tok), jnp.float32)),
        in_specs=[VMEM] * 7,
        out_specs=(VMEM, VMEM, HBM, VMEM, VMEM),
        scratch_shapes=[pltpu.VMEM((2, 2, tok, dim), jnp.float32), pltpu.VMEM((heads, tok, dim), jnp.bfloat16),
                        pltpu.SemaphoreType.DMA((heads,))],
        compiler_params=PARAMS,
        cost_estimate=pl.CostEstimate(flops=16 * tok * width * tok, bytes_accessed=3000000, transcendentals=0),
        name="away_gradients",
    )(facts, q, go, out_t, lse, kv1, kv2)


def backward(q, go, lse, row_dot, dscore, kv0, kv1, kv2, after):
    tok, width = q.shape
    dim = kv0.shape[1]
    full = jax.ShapeDtypeStruct((tok, width), jnp.bfloat16)
    return pl.pallas_call(
        backward_kernel,
        out_shape=(full, jax.ShapeDtypeStruct((2, tok, dim), jnp.float32)),
        in_specs=[VMEM] * 8 + [HBM],
        out_specs=(VMEM,) * 2,
        scratch_shapes=[pltpu.VMEM((2, tok, dim), jnp.float32)],
        compiler_params=PARAMS,
        cost_estimate=pl.CostEstimate(flops=14 * tok * width * tok, bytes_accessed=3000000, transcendentals=0),
        name="attention_backward",
    )(q, go, lse, row_dot, dscore, kv0, kv1, kv2, after)


def gram_part(facts, mine, other):
    planes, rows, cores, unit, tok = mine.shape
    feats = planes * rows * cores * unit
    chunks = 2
    return pl.pallas_call(
        gram_kernel,
        out_shape=jax.ShapeDtypeStruct((2 * rows, planes // 2, unit, feats), jnp.bfloat16),
        in_specs=[VMEM] * 3,
        out_specs=HBM,
        scratch_shapes=[pltpu.VMEM((chunks, 2 * rows, planes // 2, unit, feats // chunks), jnp.bfloat16),
                        pltpu.SemaphoreType.DMA((chunks,))],
        compiler_params=PARAMS,
        cost_estimate=pl.CostEstimate(flops=2 * feats * feats * tok, bytes_accessed=2000000, transcendentals=0),
        name="gram_part",
    )(facts, mine, other)


def row_sum(part):
    return pl.pallas_call(
        row_sum_kernel,
        out_shape=jax.ShapeDtypeStruct(part.shape[1:], part.dtype),
        in_specs=[VMEM],
        out_specs=VMEM,
        compiler_params=PARAMS,
        cost_estimate=pl.CostEstimate(flops=part.size, bytes_accessed=part.size * 2, transcendentals=0),
        name="row_sum",
    )(part)


def key_value_sum(kept, back1, back2):
    return pl.pallas_call(
        key_value_sum_kernel,
        out_shape=jax.ShapeDtypeStruct(kept.shape, jnp.bfloat16),
        in_specs=[VMEM] * 3,
        out_specs=VMEM,
        compiler_params=PARAMS,
        cost_estimate=pl.CostEstimate(flops=20 * 10**9, bytes_accessed=50 * 10**6, transcendentals=0),
        name="key_value_sum",
    )(kept, back1, back2)


CORES = 2
ROWS = 4


def shifted(block, distance, cores=range(CORES)):
    count = lax.axis_size("seq")
    return lax.ppermute(block, "seq", [(i, (i + distance) % count) for i in range(count) if i % CORES in cores])


def local(query, key_in, value_input, output_gradient, block_order):
    tok, width = query.shape
    count = lax.axis_size("seq")
    planes = count // (CORES * ROWS)
    unit = width // count
    me = lax.axis_index("seq").astype(jnp.int32)
    place = jnp.stack([me, me % CORES])
    kv0 = jnp.stack([key_in, value_input]).reshape(2 * tok, -1)
    odd2 = shifted(kv0, 2, (1,))
    even2 = shifted(kv0, 2, (0,))
    q_near, mixed, top, facts = own_block(place, block_order, query, kv0)
    core = me % CORES
    pairs = [[i, i + 1] for i in range(0, count, CORES)]
    pair = lax.all_gather(jnp.where(core == 0, kv0, odd2), "seq", axis_index_groups=pairs)
    out_t, lse, kv1, kv2 = forward(facts, even2, q_near, mixed, top, pair)
    other_t = lax.ppermute(out_t, "seq", [(i, i ^ 1) for i in range(count)])
    split = (planes, ROWS, CORES, unit, tok)
    part = gram_part(facts, out_t.reshape(split), other_t.reshape(split))
    seat = lambda z, y, c: (z * ROWS + y) * CORES + c
    near_groups = [
        [seat(2 * half + side, y, c) for side in range(2) for y in range(ROWS)]
        for half in range(planes // 2) for c in range(CORES)
    ]
    far_groups = [
        [seat(2 * half + side, y, c) for half in range(planes // 2)]
        for side in range(2) for y in range(ROWS) for c in range(CORES)
    ]
    part, lse = lax.optimization_barrier((part, lse))
    part = lax.all_to_all(part, "seq", 0, 0, axis_index_groups=near_groups, tiled=True)
    away1, away2, out, dscore, row_dot = away_gradients(facts, q_near, output_gradient, out_t, lse, kv1, kv2)
    pair = lax.all_gather(away1, "seq", axis_index_groups=pairs)
    other = jnp.where(core == 0, pair[1], pair[0])
    sent = jnp.where(core == 0, away2, away2 + other)
    back1 = jnp.where(core == 0, other, jnp.zeros_like(other))
    back2 = shifted(sent, -2)
    part = row_sum(part)
    d_query, kept = backward(q_near, output_gradient, lse, row_dot, dscore, kv0, kv1, kv2, part)
    part = lax.all_to_all(part, "seq", 0, 0, axis_index_groups=far_groups, tiled=True)
    gram = jnp.sum(part.astype(jnp.float32), axis=0) / (tok * count) ** 0.5
    return out, d_query, key_value_sum(kept, back1, back2), gram[None]


def solution(mesh):
    in_specs = (P("seq", "head"), P("seq", "head"), P("seq", "head"), P("seq", "head"), P())
    out_specs = (P("seq", "head"), P("seq", "head"), P(None, "seq", "head"), P("head", "seq", None))
    return jax.shard_map(local, mesh=mesh, in_specs=in_specs, out_specs=out_specs, check_vma=False)
```

```python
import math

import jax
import jax.numpy as jnp
from jax import lax
from jax.experimental import pallas as pl
from jax.experimental.pallas import tpu as pltpu
from jax.sharding import PartitionSpec as P

NT = (((1,), (1,)), ((), ()))
NN = (((1,), (0,)), ((), ()))
LOWEST = -1e30
VMEM_LIMIT = 16 * 1024 * 1024


def dot(a, b, dims):
    return lax.dot_general(a, b, dims, preferred_element_type=jnp.float32)


def widened(block):
    return jnp.concatenate([block, jnp.ones(block.shape, block.dtype)], 1)


def twice(block):
    return jnp.concatenate([block, block], 1)


def own_kernel(place_ref, order_ref, q_ref, kv0_ref, q_out_ref, mixed_ref, top_ref, facts_ref):
    tok, dim = kv0_ref.shape[0] // 2, kv0_ref.shape[1]
    me = place_ref[0]
    count = order_ref.shape[0]
    mine = order_ref[me]
    for step in (1, 2):
        theirs = order_ref[lax.rem(me + count - step, count)]
        hide = jnp.where(theirs <= mine, 0.0, -LOWEST).astype(jnp.float32)
        facts_ref[step - 1:step, :] = jnp.full((1, dim), hide, jnp.float32)
    facts_ref[2:3, :] = jnp.full((1, dim), place_ref[1].astype(jnp.float32), jnp.float32)
    unit = math.log2(math.e) / dim**0.5
    key = kv0_ref[:tok, :]
    value = widened(kv0_ref[tok:, :])
    causal = lax.broadcasted_iota(jnp.int32, (tok, tok), 1) <= lax.broadcasted_iota(jnp.int32, (tok, tok), 0)
    q_out_ref[...] = q_ref[...]
    for h in range(q_ref.shape[1] // dim):
        scores = jnp.where(causal, dot(q_ref[:, h * dim:(h + 1) * dim], key, NT), LOWEST)
        top = jnp.max(scores, axis=1, keepdims=True) * unit
        expo = jnp.exp2(scores * unit - top)
        mixed_ref[h] = dot(expo.astype(jnp.bfloat16), value, NN)
        top_ref[h] = jnp.broadcast_to(top, (tok, dim))


def merged(scores, own, hide, mixed, value, unit):
    top = jnp.maximum(own, jnp.max(scores, axis=1, keepdims=True) * unit - hide)
    expo = jnp.exp2(scores * unit - twice(top + hide))
    return top, mixed * twice(jnp.exp2(own - top)) + dot(expo.astype(jnp.bfloat16), value, NN)


def next_kernel(facts_ref, q_ref, mixed_ref, top_ref, pair_ref, mixed_out_ref, top_out_ref, kv1_ref):
    heads, tok, dim = top_ref.shape
    unit = math.log2(math.e) / dim**0.5
    core = facts_ref[2:3, :1].astype(jnp.bfloat16)
    kv1 = pair_ref[0] * core + pair_ref[1] * (1 - core)
    kv1_ref[...] = kv1
    key, value = kv1[:tok], widened(kv1[tok:])
    for h in range(heads):
        scores = dot(q_ref[:, h * dim:(h + 1) * dim], key, NT)
        top_out_ref[h], mixed_out_ref[h] = merged(scores, top_ref[h], facts_ref[0:1, :], mixed_ref[h], value, unit)


def last_kernel(facts_ref, even2_ref, q_ref, mixed_ref, top_ref, pair_ref, out_t_ref, lse_ref, kv2_ref):
    heads, tok, dim = top_ref.shape
    unit = math.log2(math.e) / dim**0.5
    core = facts_ref[2:3, :1].astype(jnp.bfloat16)
    kv2 = pair_ref[1] * core + even2_ref[...] * (1 - core)
    kv2_ref[...] = kv2
    key, value = kv2[:tok], widened(kv2[tok:])
    for h in range(heads):
        cols = slice(h * dim, (h + 1) * dim)
        scores = dot(q_ref[:, cols], key, NT)
        top, mixed = merged(scores, top_ref[h], facts_ref[1:2, :], mixed_ref[h], value, unit)
        total = mixed[:, dim:]
        out_t_ref[cols, :] = (mixed[:, :dim] / total).T.astype(jnp.bfloat16)
        lse_ref[h:h + 1, :] = (top + jnp.log2(total)).T[:1]


def away_kernel(facts_ref, q_ref, go_ref, out_t_ref, lse_ref, kv1_ref, kv2_ref, away1_ref, away2_ref, out_hbm, dscore_ref,
                row_dot_ref, acc_ref, out_ref, sems):
    heads, _, tok, _ = dscore_ref.shape
    dim = kv1_ref.shape[1]
    scale = 1.0 / dim**0.5
    unit = math.log2(math.e) * scale
    hide = [twice(facts_ref[j:j + 1, :]) for j in range(2)]
    saves = [pltpu.make_async_copy(out_ref.at[h], out_hbm.at[:, pl.ds(h * dim, dim)], sems.at[h]) for h in range(heads)]
    keys = [kv_ref[:tok, :] for kv_ref in (kv1_ref, kv2_ref)]
    values = [kv_ref[tok:, :] for kv_ref in (kv1_ref, kv2_ref)]
    for h in range(heads):
        cols = slice(h * dim, (h + 1) * dim)
        qh = q_ref[:, cols]
        gh = go_ref[:, cols]
        out_t = out_t_ref[cols, :].astype(jnp.float32)
        row_dot = jnp.sum(gh.astype(jnp.float32).T * out_t, axis=0, keepdims=True)
        row_dot_ref[h:h + 1, :] = row_dot
        out_ref[h] = out_t.T.astype(jnp.bfloat16)
        saves[h].start()
        for j in range(2):
            weights = jnp.exp2(dot(keys[j], qh, NT) * unit - (lse_ref[h:h + 1, :] + hide[j]))
            dscore = (weights * (dot(values[j], gh, NT) - row_dot)).astype(jnp.bfloat16)
            dscore_ref[h, j] = dscore
            dk = dot(dscore, qh, NN)
            dv = dot(weights.astype(jnp.bfloat16), gh, NN)
            if h > 0:
                dk = acc_ref[j, 0] + dk
                dv = acc_ref[j, 1] + dv
            if h < heads - 1:
                acc_ref[j, 0] = dk
                acc_ref[j, 1] = dv
            else:
                away_ref = (away1_ref, away2_ref)[j]
                away_ref[0] = (dk * scale).astype(away_ref.dtype)
                away_ref[1] = dv.astype(away_ref.dtype)
    for save in saves:
        save.wait()


def backward_kernel(q_ref, go_ref, lse_ref, row_dot_ref, dscore_ref, kv0_ref, kv1_ref, kv2_ref, after_ref, dq_ref, kept_ref, acc_ref):
    heads, _, tok, _ = dscore_ref.shape
    dim = kv0_ref.shape[1]
    scale = 1.0 / dim**0.5
    unit = math.log2(math.e) * scale
    key = kv0_ref[:tok, :]
    value = kv0_ref[tok:, :]
    keys_t = [kv_ref[:tok, :].T for kv_ref in (kv0_ref, kv1_ref, kv2_ref)]
    causal = lax.broadcasted_iota(jnp.int32, (tok, tok), 0) <= lax.broadcasted_iota(jnp.int32, (tok, tok), 1)
    for h in range(heads):
        cols = slice(h * dim, (h + 1) * dim)
        qh = q_ref[:, cols]
        gh = go_ref[:, cols]
        scores = jnp.where(causal, dot(key, qh, NT), LOWEST)
        weights = jnp.exp2(scores * unit - lse_ref[h:h + 1, :])
        dscore = (weights * (dot(value, gh, NT) - row_dot_ref[h:h + 1, :])).astype(jnp.bfloat16)
        dq_t = dot(keys_t[0], dscore, NN)
        for j in range(2):
            dq_t = dq_t + dot(keys_t[j + 1], dscore_ref[h, j], NN)
        dq_ref[:, cols] = (dq_t * scale).T.astype(jnp.bfloat16)
        dk = dot(dscore, qh, NN)
        dv = dot(weights.astype(jnp.bfloat16), gh, NN)
        if h > 0:
            dk = acc_ref[0] + dk
            dv = acc_ref[1] + dv
        if h < heads - 1:
            acc_ref[0] = dk
            acc_ref[1] = dv
        else:
            kept_ref[0] = dk * scale
            kept_ref[1] = dv


def gram_kernel(facts_ref, mine_ref, other_ref, part_hbm, part_ref, sems):
    core = facts_ref[2:3, :1].astype(jnp.bfloat16)
    planes, rows, cores, unit, tok = mine_ref.shape
    chunks = part_ref.shape[0]
    step = planes // chunks
    wide = step * rows * cores * unit
    picked = [ref[:, :, 0] * (1 - core) + ref[:, :, 1] * core for ref in (mine_ref, other_ref)]
    left = jnp.concatenate([block.reshape(planes * rows * unit, tok) for block in picked], axis=1)
    saves = []
    for i in range(chunks):
        right = jnp.concatenate(
            [ref[i * step:(i + 1) * step].reshape(wide, tok) for ref in (mine_ref, other_ref)], axis=1
        )
        got = dot(left, right, NT).astype(jnp.bfloat16)
        for plane in range(planes):
            block = got[plane * rows * unit:(plane + 1) * rows * unit]
            first = (plane % 2) * rows
            part_ref[i, first:first + rows, plane // 2] = block.reshape(rows, unit, wide)
        save = pltpu.make_async_copy(part_ref.at[i], part_hbm.at[:, :, :, pl.ds(i * wide, wide)], sems.at[i])
        save.start()
        saves.append(save)
    for save in saves:
        save.wait()


def row_sum_kernel(part_ref, sum_ref):
    total = part_ref[0].astype(jnp.float32)
    for i in range(1, part_ref.shape[0]):
        total = total + part_ref[i].astype(jnp.float32)
    sum_ref[...] = total.astype(sum_ref.dtype)


def key_value_sum_kernel(kept_ref, back1_ref, back2_ref, total_ref):
    total = kept_ref[...] + back1_ref[...].astype(jnp.float32) + back2_ref[...].astype(jnp.float32)
    total_ref[...] = total.astype(total_ref.dtype)


SMEM = pl.BlockSpec(memory_space=pltpu.SMEM)
VMEM = pl.BlockSpec(memory_space=pltpu.VMEM)
HBM = pl.BlockSpec(memory_space=pltpu.HBM)
PARAMS = pltpu.CompilerParams(vmem_limit_bytes=VMEM_LIMIT)


def own_block(place, order, q, kv0):
    tok, width = q.shape
    dim = kv0.shape[1]
    heads = width // dim
    return pl.pallas_call(
        own_kernel,
        out_shape=(jax.ShapeDtypeStruct(q.shape, q.dtype), jax.ShapeDtypeStruct((heads, tok, 2 * dim), jnp.float32),
                   jax.ShapeDtypeStruct((heads, tok, dim), jnp.float32), jax.ShapeDtypeStruct((8, dim), jnp.float32)),
        in_specs=[SMEM] * 2 + [VMEM] * 2,
        out_specs=(VMEM,) * 4,
        compiler_params=PARAMS,
        cost_estimate=pl.CostEstimate(flops=4 * tok * width * tok, bytes_accessed=6000000, transcendentals=0),
        name="own_block",
    )(place, order, q, kv0)


def next_block(facts, q, mixed, top, pair):
    tok, width = q.shape
    return pl.pallas_call(
        next_kernel,
        out_shape=(jax.ShapeDtypeStruct(mixed.shape, mixed.dtype), jax.ShapeDtypeStruct(top.shape, top.dtype),
                   jax.ShapeDtypeStruct(pair.shape[1:], pair.dtype)),
        in_specs=[VMEM] * 5,
        out_specs=(VMEM,) * 3,
        compiler_params=PARAMS,
        cost_estimate=pl.CostEstimate(flops=4 * tok * width * tok, bytes_accessed=2000000, transcendentals=0),
        name="next_block",
    )(facts, q, mixed, top, pair)


def last_block(facts, even2, q, mixed, top, pair):
    tok, width = q.shape
    heads = top.shape[0]
    return pl.pallas_call(
        last_kernel,
        out_shape=(jax.ShapeDtypeStruct((width, tok), jnp.bfloat16), jax.ShapeDtypeStruct((heads, tok), jnp.float32),
                   jax.ShapeDtypeStruct(even2.shape, even2.dtype)),
        in_specs=[VMEM] * 6,
        out_specs=(VMEM,) * 3,
        compiler_params=PARAMS,
        cost_estimate=pl.CostEstimate(flops=4 * tok * width * tok, bytes_accessed=2000000, transcendentals=0),
        name="last_block",
    )(facts, even2, q, mixed, top, pair)


def away_gradients(facts, q, go, out_t, lse, kv1, kv2):
    tok, width = q.shape
    dim = kv1.shape[1]
    heads = width // dim
    pair = jax.ShapeDtypeStruct((2, tok, dim), jnp.bfloat16)
    return pl.pallas_call(
        away_kernel,
        out_shape=(pair, pair, jax.ShapeDtypeStruct((tok, width), jnp.bfloat16),
                   jax.ShapeDtypeStruct((heads, 2, tok, tok), jnp.bfloat16), jax.ShapeDtypeStruct((heads, tok), jnp.float32)),
        in_specs=[VMEM] * 7,
        out_specs=(VMEM, VMEM, HBM, VMEM, VMEM),
        scratch_shapes=[pltpu.VMEM((2, 2, tok, dim), jnp.float32), pltpu.VMEM((heads, tok, dim), jnp.bfloat16),
                        pltpu.SemaphoreType.DMA((heads,))],
        compiler_params=PARAMS,
        cost_estimate=pl.CostEstimate(flops=16 * tok * width * tok, bytes_accessed=3000000, transcendentals=0),
        name="away_gradients",
    )(facts, q, go, out_t, lse, kv1, kv2)


def backward(q, go, lse, row_dot, dscore, kv0, kv1, kv2, after):
    tok, width = q.shape
    dim = kv0.shape[1]
    full = jax.ShapeDtypeStruct((tok, width), jnp.bfloat16)
    return pl.pallas_call(
        backward_kernel,
        out_shape=(full, jax.ShapeDtypeStruct((2, tok, dim), jnp.float32)),
        in_specs=[VMEM] * 8 + [HBM],
        out_specs=(VMEM,) * 2,
        scratch_shapes=[pltpu.VMEM((2, tok, dim), jnp.float32)],
        compiler_params=PARAMS,
        cost_estimate=pl.CostEstimate(flops=14 * tok * width * tok, bytes_accessed=3000000, transcendentals=0),
        name="attention_backward",
    )(q, go, lse, row_dot, dscore, kv0, kv1, kv2, after)


def gram_part(facts, mine, other):
    planes, rows, cores, unit, tok = mine.shape
    feats = planes * rows * cores * unit
    chunks = 2
    return pl.pallas_call(
        gram_kernel,
        out_shape=jax.ShapeDtypeStruct((2 * rows, planes // 2, unit, feats), jnp.bfloat16),
        in_specs=[VMEM] * 3,
        out_specs=HBM,
        scratch_shapes=[pltpu.VMEM((chunks, 2 * rows, planes // 2, unit, feats // chunks), jnp.bfloat16),
                        pltpu.SemaphoreType.DMA((chunks,))],
        compiler_params=PARAMS,
        cost_estimate=pl.CostEstimate(flops=2 * feats * feats * tok, bytes_accessed=2000000, transcendentals=0),
        name="gram_part",
    )(facts, mine, other)


def row_sum(part):
    return pl.pallas_call(
        row_sum_kernel,
        out_shape=jax.ShapeDtypeStruct(part.shape[1:], part.dtype),
        in_specs=[VMEM],
        out_specs=VMEM,
        compiler_params=PARAMS,
        cost_estimate=pl.CostEstimate(flops=part.size, bytes_accessed=part.size * 2, transcendentals=0),
        name="row_sum",
    )(part)


def key_value_sum(kept, back1, back2):
    return pl.pallas_call(
        key_value_sum_kernel,
        out_shape=jax.ShapeDtypeStruct(kept.shape, jnp.bfloat16),
        in_specs=[VMEM] * 3,
        out_specs=VMEM,
        compiler_params=PARAMS,
        cost_estimate=pl.CostEstimate(flops=20 * 10**9, bytes_accessed=50 * 10**6, transcendentals=0),
        name="key_value_sum",
    )(kept, back1, back2)


CORES = 2
ROWS = 4


def shifted(block, distance, cores=range(CORES)):
    count = lax.axis_size("seq")
    return lax.ppermute(block, "seq", [(i, (i + distance) % count) for i in range(count) if i % CORES in cores])


def local(query, key_in, value_input, output_gradient, block_order):
    tok, width = query.shape
    count = lax.axis_size("seq")
    planes = count // (CORES * ROWS)
    unit = width // count
    me = lax.axis_index("seq").astype(jnp.int32)
    place = jnp.stack([me, me % CORES])
    kv0 = jnp.stack([key_in, value_input]).reshape(2 * tok, -1)
    odd2 = shifted(kv0, 2, (1,))
    even2 = shifted(kv0, 2, (0,))
    q_near, mixed, top, facts = own_block(place, block_order, query, kv0)
    core = me % CORES
    pairs = [[i, i + 1] for i in range(0, count, CORES)]
    pair = lax.all_gather(jnp.where(core == 0, kv0, odd2), "seq", axis_index_groups=pairs)
    mixed, top, kv1 = next_block(facts, q_near, mixed, top, pair)
    out_t, lse, kv2 = last_block(facts, even2, q_near, mixed, top, pair)
    other_t = lax.ppermute(out_t, "seq", [(i, i ^ 1) for i in range(count)])
    split = (planes, ROWS, CORES, unit, tok)
    part = gram_part(facts, out_t.reshape(split), other_t.reshape(split))
    seat = lambda z, y, c: (z * ROWS + y) * CORES + c
    near_groups = [
        [seat(2 * half + side, y, c) for side in range(2) for y in range(ROWS)]
        for half in range(planes // 2) for c in range(CORES)
    ]
    far_groups = [
        [seat(2 * half + side, y, c) for half in range(planes // 2)]
        for side in range(2) for y in range(ROWS) for c in range(CORES)
    ]
    part, lse = lax.optimization_barrier((part, lse))
    part = lax.all_to_all(part, "seq", 0, 0, axis_index_groups=near_groups, tiled=True)
    away1, away2, out, dscore, row_dot = away_gradients(facts, q_near, output_gradient, out_t, lse, kv1, kv2)
    pair = lax.all_gather(away1, "seq", axis_index_groups=pairs)
    other = jnp.where(core == 0, pair[1], pair[0])
    sent = jnp.where(core == 0, away2, away2 + other)
    back1 = jnp.where(core == 0, other, jnp.zeros_like(other))
    back2 = shifted(sent, -2)
    part = row_sum(part)
    d_query, kept = backward(q_near, output_gradient, lse, row_dot, dscore, kv0, kv1, kv2, part)
    part = lax.all_to_all(part, "seq", 0, 0, axis_index_groups=far_groups, tiled=True)
    gram = jnp.sum(part.astype(jnp.float32), axis=0) / (tok * count) ** 0.5
    return out, d_query, key_value_sum(kept, back1, back2), gram[None]


def solution(mesh):
    in_specs = (P("seq", "head"), P("seq", "head"), P("seq", "head"), P("seq", "head"), P())
    out_specs = (P("seq", "head"), P("seq", "head"), P(None, "seq", "head"), P("head", "seq", None))
    return jax.shard_map(local, mesh=mesh, in_specs=in_specs, out_specs=out_specs, check_vma=False)
```

```python
import math

import jax
import jax.numpy as jnp
from jax import lax
from jax.experimental import pallas as pl
from jax.experimental.pallas import tpu as pltpu
from jax.sharding import PartitionSpec as P

NT = (((1,), (1,)), ((), ()))
NN = (((1,), (0,)), ((), ()))
LOWEST = -1e30
VMEM_LIMIT = 16 * 1024 * 1024


def dot(a, b, dims):
    return lax.dot_general(a, b, dims, preferred_element_type=jnp.float32)


def widened(block):
    return jnp.concatenate([block, jnp.ones(block.shape, block.dtype)], 1)


def twice(block):
    return jnp.concatenate([block, block], 1)


def own_kernel(place_ref, order_ref, q_ref, kv0_ref, q_out_ref, mixed_ref, top_ref, facts_ref):
    tok, dim = kv0_ref.shape[0] // 2, kv0_ref.shape[1]
    me = place_ref[0]
    count = order_ref.shape[0]
    mine = order_ref[me]
    for step in (1, 2):
        theirs = order_ref[lax.rem(me + count - step, count)]
        hide = jnp.where(theirs <= mine, 0.0, -LOWEST).astype(jnp.float32)
        facts_ref[step - 1:step, :] = jnp.full((1, dim), hide, jnp.float32)
    facts_ref[2:3, :] = jnp.full((1, dim), place_ref[1].astype(jnp.float32), jnp.float32)
    unit = math.log2(math.e) / dim**0.5
    key = kv0_ref[:tok, :]
    value = widened(kv0_ref[tok:, :])
    causal = lax.broadcasted_iota(jnp.int32, (tok, tok), 1) <= lax.broadcasted_iota(jnp.int32, (tok, tok), 0)
    q_out_ref[...] = q_ref[...]
    for h in range(q_ref.shape[1] // dim):
        scores = jnp.where(causal, dot(q_ref[:, h * dim:(h + 1) * dim], key, NT), LOWEST)
        top = jnp.max(scores, axis=1, keepdims=True) * unit
        expo = jnp.exp2(scores * unit - top)
        mixed_ref[h] = dot(expo.astype(jnp.bfloat16), value, NN)
        top_ref[h] = jnp.broadcast_to(top, (tok, dim))


def merged(scores, own, hide, mixed, value, unit):
    top = jnp.maximum(own, jnp.max(scores, axis=1, keepdims=True) * unit - hide)
    expo = jnp.exp2(scores * unit - twice(top + hide))
    return top, mixed * twice(jnp.exp2(own - top)) + dot(expo.astype(jnp.bfloat16), value, NN)


def next_kernel(facts_ref, q_ref, mixed_ref, top_ref, pair_ref, mixed_out_ref, top_out_ref, kv1_ref):
    heads, tok, dim = top_ref.shape
    unit = math.log2(math.e) / dim**0.5
    core = facts_ref[2:3, :1].astype(jnp.bfloat16)
    kv1 = pair_ref[0] * core + pair_ref[1] * (1 - core)
    kv1_ref[...] = kv1
    key, value = kv1[:tok], widened(kv1[tok:])
    for h in range(heads):
        scores = dot(q_ref[:, h * dim:(h + 1) * dim], key, NT)
        top_out_ref[h], mixed_out_ref[h] = merged(scores, top_ref[h], facts_ref[0:1, :], mixed_ref[h], value, unit)


def last_kernel(facts_ref, even2_ref, q_ref, mixed_ref, top_ref, pair_ref, out_t_ref, lse_ref, kv2_ref):
    heads, tok, dim = top_ref.shape
    unit = math.log2(math.e) / dim**0.5
    core = facts_ref[2:3, :1].astype(jnp.bfloat16)
    kv2 = pair_ref[1] * core + even2_ref[...] * (1 - core)
    kv2_ref[...] = kv2
    key, value = kv2[:tok], widened(kv2[tok:])
    for h in range(heads):
        cols = slice(h * dim, (h + 1) * dim)
        scores = dot(q_ref[:, cols], key, NT)
        top, mixed = merged(scores, top_ref[h], facts_ref[1:2, :], mixed_ref[h], value, unit)
        total = mixed[:, dim:]
        out_t_ref[cols, :] = (mixed[:, :dim] / total).T.astype(jnp.bfloat16)
        lse_ref[h:h + 1, :] = (top + jnp.log2(total)).T[:1]


def away_kernel(facts_ref, q_ref, go_ref, out_t_ref, lse_ref, kv1_ref, kv2_ref, away1_ref, away2_ref, out_hbm, dscore_ref,
                row_dot_ref, acc_ref, out_ref, sems):
    heads, _, tok, _ = dscore_ref.shape
    dim = kv1_ref.shape[1]
    scale = 1.0 / dim**0.5
    unit = math.log2(math.e) * scale
    hide = [twice(facts_ref[j:j + 1, :]) for j in range(2)]
    saves = [pltpu.make_async_copy(out_ref.at[h], out_hbm.at[:, pl.ds(h * dim, dim)], sems.at[h]) for h in range(heads)]
    keys = [kv_ref[:tok, :] for kv_ref in (kv1_ref, kv2_ref)]
    values = [kv_ref[tok:, :] for kv_ref in (kv1_ref, kv2_ref)]
    for h in range(heads):
        cols = slice(h * dim, (h + 1) * dim)
        qh = q_ref[:, cols]
        gh = go_ref[:, cols]
        out_t = out_t_ref[cols, :].astype(jnp.float32)
        row_dot = jnp.sum(gh.astype(jnp.float32).T * out_t, axis=0, keepdims=True)
        row_dot_ref[h:h + 1, :] = row_dot
        out_ref[h] = out_t.T.astype(jnp.bfloat16)
        saves[h].start()
        for j in range(2):
            weights = jnp.exp2(dot(keys[j], qh, NT) * unit - (lse_ref[h:h + 1, :] + hide[j]))
            dscore = (weights * (dot(values[j], gh, NT) - row_dot)).astype(jnp.bfloat16)
            dscore_ref[h, j] = dscore
            dk = dot(dscore, qh, NN)
            dv = dot(weights.astype(jnp.bfloat16), gh, NN)
            if h > 0:
                dk = acc_ref[j, 0] + dk
                dv = acc_ref[j, 1] + dv
            if h < heads - 1:
                acc_ref[j, 0] = dk
                acc_ref[j, 1] = dv
            else:
                away_ref = (away1_ref, away2_ref)[j]
                away_ref[0] = (dk * scale).astype(away_ref.dtype)
                away_ref[1] = dv.astype(away_ref.dtype)
    for save in saves:
        save.wait()


def backward_kernel(q_ref, go_ref, lse_ref, row_dot_ref, dscore_ref, kv0_ref, kv1_ref, kv2_ref, after_ref, dq_ref, kept_ref, acc_ref):
    heads, _, tok, _ = dscore_ref.shape
    dim = kv0_ref.shape[1]
    scale = 1.0 / dim**0.5
    unit = math.log2(math.e) * scale
    key = kv0_ref[:tok, :]
    value = kv0_ref[tok:, :]
    keys_t = [kv_ref[:tok, :].T for kv_ref in (kv0_ref, kv1_ref, kv2_ref)]
    causal = lax.broadcasted_iota(jnp.int32, (tok, tok), 0) <= lax.broadcasted_iota(jnp.int32, (tok, tok), 1)
    for h in range(heads):
        cols = slice(h * dim, (h + 1) * dim)
        qh = q_ref[:, cols]
        gh = go_ref[:, cols]
        scores = jnp.where(causal, dot(key, qh, NT), LOWEST)
        weights = jnp.exp2(scores * unit - lse_ref[h:h + 1, :])
        dscore = (weights * (dot(value, gh, NT) - row_dot_ref[h:h + 1, :])).astype(jnp.bfloat16)
        dq_t = dot(keys_t[0], dscore, NN)
        for j in range(2):
            dq_t = dq_t + dot(keys_t[j + 1], dscore_ref[h, j], NN)
        dq_ref[:, cols] = (dq_t * scale).T.astype(jnp.bfloat16)
        dk = dot(dscore, qh, NN)
        dv = dot(weights.astype(jnp.bfloat16), gh, NN)
        if h > 0:
            dk = acc_ref[0] + dk
            dv = acc_ref[1] + dv
        if h < heads - 1:
            acc_ref[0] = dk
            acc_ref[1] = dv
        else:
            kept_ref[0] = dk * scale
            kept_ref[1] = dv


def picked(facts_ref, ref):
    planes, rows, _, unit, tok = ref.shape
    core = facts_ref[2:3, :1].astype(jnp.bfloat16)
    return (ref[:, :, 0] * (1 - core) + ref[:, :, 1] * core).reshape(planes * rows * unit, tok)


def own_gram_kernel(facts_ref, mine_ref, own_ref):
    planes, rows, cores, unit, tok = mine_ref.shape
    chunks = own_ref.shape[0]
    step = planes // chunks
    left = picked(facts_ref, mine_ref)
    for i in range(chunks):
        own_ref[i] = dot(left, mine_ref[i * step:(i + 1) * step].reshape(step * rows * cores * unit, tok), NT)


def gram_kernel(facts_ref, own_ref, other_ref, part_hbm, part_ref, sems):
    planes, rows, cores, unit, tok = other_ref.shape
    chunks = part_ref.shape[0]
    step = planes // chunks
    wide = step * rows * cores * unit
    left = picked(facts_ref, other_ref)
    saves = []
    for i in range(chunks):
        right = other_ref[i * step:(i + 1) * step].reshape(wide, tok)
        got = (own_ref[i] + dot(left, right, NT)).astype(jnp.bfloat16)
        for plane in range(planes):
            block = got[plane * rows * unit:(plane + 1) * rows * unit]
            first = (plane % 2) * rows
            part_ref[i, first:first + rows, plane // 2] = block.reshape(rows, unit, wide)
        save = pltpu.make_async_copy(part_ref.at[i], part_hbm.at[:, :, :, pl.ds(i * wide, wide)], sems.at[i])
        save.start()
        saves.append(save)
    for save in saves:
        save.wait()


def row_sum_kernel(part_ref, sum_ref):
    total = part_ref[0].astype(jnp.float32)
    for i in range(1, part_ref.shape[0]):
        total = total + part_ref[i].astype(jnp.float32)
    sum_ref[...] = total.astype(sum_ref.dtype)


def key_value_sum_kernel(kept_ref, back1_ref, back2_ref, total_ref):
    total = kept_ref[...] + back1_ref[...].astype(jnp.float32) + back2_ref[...].astype(jnp.float32)
    total_ref[...] = total.astype(total_ref.dtype)


SMEM = pl.BlockSpec(memory_space=pltpu.SMEM)
VMEM = pl.BlockSpec(memory_space=pltpu.VMEM)
HBM = pl.BlockSpec(memory_space=pltpu.HBM)
PARAMS = pltpu.CompilerParams(vmem_limit_bytes=VMEM_LIMIT)


def own_block(place, order, q, kv0):
    tok, width = q.shape
    dim = kv0.shape[1]
    heads = width // dim
    return pl.pallas_call(
        own_kernel,
        out_shape=(jax.ShapeDtypeStruct(q.shape, q.dtype), jax.ShapeDtypeStruct((heads, tok, 2 * dim), jnp.float32),
                   jax.ShapeDtypeStruct((heads, tok, dim), jnp.float32), jax.ShapeDtypeStruct((8, dim), jnp.float32)),
        in_specs=[SMEM] * 2 + [VMEM] * 2,
        out_specs=(VMEM,) * 4,
        compiler_params=PARAMS,
        cost_estimate=pl.CostEstimate(flops=4 * tok * width * tok, bytes_accessed=6000000, transcendentals=0),
        name="own_block",
    )(place, order, q, kv0)


def next_block(facts, q, mixed, top, pair):
    tok, width = q.shape
    return pl.pallas_call(
        next_kernel,
        out_shape=(jax.ShapeDtypeStruct(mixed.shape, mixed.dtype), jax.ShapeDtypeStruct(top.shape, top.dtype),
                   jax.ShapeDtypeStruct(pair.shape[1:], pair.dtype)),
        in_specs=[VMEM] * 5,
        out_specs=(VMEM,) * 3,
        compiler_params=PARAMS,
        cost_estimate=pl.CostEstimate(flops=4 * tok * width * tok, bytes_accessed=2000000, transcendentals=0),
        name="next_block",
    )(facts, q, mixed, top, pair)


def last_block(facts, even2, q, mixed, top, pair):
    tok, width = q.shape
    heads = top.shape[0]
    return pl.pallas_call(
        last_kernel,
        out_shape=(jax.ShapeDtypeStruct((width, tok), jnp.bfloat16), jax.ShapeDtypeStruct((heads, tok), jnp.float32),
                   jax.ShapeDtypeStruct(even2.shape, even2.dtype)),
        in_specs=[VMEM] * 6,
        out_specs=(VMEM,) * 3,
        compiler_params=PARAMS,
        cost_estimate=pl.CostEstimate(flops=4 * tok * width * tok, bytes_accessed=2000000, transcendentals=0),
        name="last_block",
    )(facts, even2, q, mixed, top, pair)


def away_gradients(facts, q, go, out_t, lse, kv1, kv2):
    tok, width = q.shape
    dim = kv1.shape[1]
    heads = width // dim
    pair = jax.ShapeDtypeStruct((2, tok, dim), jnp.bfloat16)
    return pl.pallas_call(
        away_kernel,
        out_shape=(pair, pair, jax.ShapeDtypeStruct((tok, width), jnp.bfloat16),
                   jax.ShapeDtypeStruct((heads, 2, tok, tok), jnp.bfloat16), jax.ShapeDtypeStruct((heads, tok), jnp.float32)),
        in_specs=[VMEM] * 7,
        out_specs=(VMEM, VMEM, HBM, VMEM, VMEM),
        scratch_shapes=[pltpu.VMEM((2, 2, tok, dim), jnp.float32), pltpu.VMEM((heads, tok, dim), jnp.bfloat16),
                        pltpu.SemaphoreType.DMA((heads,))],
        compiler_params=PARAMS,
        cost_estimate=pl.CostEstimate(flops=16 * tok * width * tok, bytes_accessed=3000000, transcendentals=0),
        name="away_gradients",
    )(facts, q, go, out_t, lse, kv1, kv2)


def backward(q, go, lse, row_dot, dscore, kv0, kv1, kv2, after):
    tok, width = q.shape
    dim = kv0.shape[1]
    full = jax.ShapeDtypeStruct((tok, width), jnp.bfloat16)
    return pl.pallas_call(
        backward_kernel,
        out_shape=(full, jax.ShapeDtypeStruct((2, tok, dim), jnp.float32)),
        in_specs=[VMEM] * 8 + [HBM],
        out_specs=(VMEM,) * 2,
        scratch_shapes=[pltpu.VMEM((2, tok, dim), jnp.float32)],
        compiler_params=PARAMS,
        cost_estimate=pl.CostEstimate(flops=14 * tok * width * tok, bytes_accessed=3000000, transcendentals=0),
        name="attention_backward",
    )(q, go, lse, row_dot, dscore, kv0, kv1, kv2, after)


def own_gram(facts, mine):
    planes, rows, cores, unit, tok = mine.shape
    feats = planes * rows * cores * unit
    return pl.pallas_call(
        own_gram_kernel,
        out_shape=jax.ShapeDtypeStruct((2, feats // cores, feats // 2), jnp.float32),
        in_specs=[VMEM] * 2,
        out_specs=VMEM,
        compiler_params=PARAMS,
        cost_estimate=pl.CostEstimate(flops=feats * feats * tok, bytes_accessed=2000000, transcendentals=0),
        name="own_gram",
    )(facts, mine)


def gram_part(facts, own, other):
    planes, rows, cores, unit, tok = other.shape
    feats = planes * rows * cores * unit
    chunks = own.shape[0]
    return pl.pallas_call(
        gram_kernel,
        out_shape=jax.ShapeDtypeStruct((2 * rows, planes // 2, unit, feats), jnp.bfloat16),
        in_specs=[VMEM] * 3,
        out_specs=HBM,
        scratch_shapes=[pltpu.VMEM((chunks, 2 * rows, planes // 2, unit, feats // chunks), jnp.bfloat16),
                        pltpu.SemaphoreType.DMA((chunks,))],
        compiler_params=PARAMS,
        cost_estimate=pl.CostEstimate(flops=feats * feats * tok, bytes_accessed=2000000, transcendentals=0),
        name="gram_part",
    )(facts, own, other)


def row_sum(part):
    return pl.pallas_call(
        row_sum_kernel,
        out_shape=jax.ShapeDtypeStruct(part.shape[1:], part.dtype),
        in_specs=[VMEM],
        out_specs=VMEM,
        compiler_params=PARAMS,
        cost_estimate=pl.CostEstimate(flops=part.size, bytes_accessed=part.size * 2, transcendentals=0),
        name="row_sum",
    )(part)


def key_value_sum(kept, back1, back2):
    return pl.pallas_call(
        key_value_sum_kernel,
        out_shape=jax.ShapeDtypeStruct(kept.shape, jnp.bfloat16),
        in_specs=[VMEM] * 3,
        out_specs=VMEM,
        compiler_params=PARAMS,
        cost_estimate=pl.CostEstimate(flops=20 * 10**9, bytes_accessed=50 * 10**6, transcendentals=0),
        name="key_value_sum",
    )(kept, back1, back2)


CORES = 2
ROWS = 4


def shifted(block, distance, cores=range(CORES)):
    count = lax.axis_size("seq")
    return lax.ppermute(block, "seq", [(i, (i + distance) % count) for i in range(count) if i % CORES in cores])


def local(query, key_in, value_input, output_gradient, block_order):
    tok, width = query.shape
    count = lax.axis_size("seq")
    planes = count // (CORES * ROWS)
    unit = width // count
    me = lax.axis_index("seq").astype(jnp.int32)
    place = jnp.stack([me, me % CORES])
    kv0 = jnp.stack([key_in, value_input]).reshape(2 * tok, -1)
    odd2 = shifted(kv0, 2, (1,))
    even2 = shifted(kv0, 2, (0,))
    q_near, mixed, top, facts = own_block(place, block_order, query, kv0)
    core = me % CORES
    pairs = [[i, i + 1] for i in range(0, count, CORES)]
    pair = lax.all_gather(jnp.where(core == 0, kv0, odd2), "seq", axis_index_groups=pairs)
    mixed, top, kv1 = next_block(facts, q_near, mixed, top, pair)
    out_t, lse, kv2 = last_block(facts, even2, q_near, mixed, top, pair)
    other_t = lax.ppermute(out_t, "seq", [(i, i ^ 1) for i in range(count)])
    split = (planes, ROWS, CORES, unit, tok)
    part = gram_part(facts, own_gram(facts, out_t.reshape(split)), other_t.reshape(split))
    seat = lambda z, y, c: (z * ROWS + y) * CORES + c
    near_groups = [
        [seat(2 * half + side, y, c) for side in range(2) for y in range(ROWS)]
        for half in range(planes // 2) for c in range(CORES)
    ]
    far_groups = [
        [seat(2 * half + side, y, c) for half in range(planes // 2)]
        for side in range(2) for y in range(ROWS) for c in range(CORES)
    ]
    part, lse = lax.optimization_barrier((part, lse))
    part = lax.all_to_all(part, "seq", 0, 0, axis_index_groups=near_groups, tiled=True)
    away1, away2, out, dscore, row_dot = away_gradients(facts, q_near, output_gradient, out_t, lse, kv1, kv2)
    pair = lax.all_gather(away1, "seq", axis_index_groups=pairs)
    other = jnp.where(core == 0, pair[1], pair[0])
    sent = jnp.where(core == 0, away2, away2 + other)
    back1 = jnp.where(core == 0, other, jnp.zeros_like(other))
    back2 = shifted(sent, -2)
    part = row_sum(part)
    d_query, kept = backward(q_near, output_gradient, lse, row_dot, dscore, kv0, kv1, kv2, part)
    part = lax.all_to_all(part, "seq", 0, 0, axis_index_groups=far_groups, tiled=True)
    gram = jnp.sum(part.astype(jnp.float32), axis=0) / (tok * count) ** 0.5
    return out, d_query, key_value_sum(kept, back1, back2), gram[None]


def solution(mesh):
    in_specs = (P("seq", "head"), P("seq", "head"), P("seq", "head"), P("seq", "head"), P())
    out_specs = (P("seq", "head"), P("seq", "head"), P(None, "seq", "head"), P("head", "seq", None))
    return jax.shard_map(local, mesh=mesh, in_specs=in_specs, out_specs=out_specs, check_vma=False)
```
